256 devices in a mesh: row: 8 (over y_hi, x), col: 32 (over y_lo, z, core).
Axes of the slice: x: 4, y: 4 (y_hi: 2, y_lo: 2; y = y_hi * 2 + y_lo), z: 8, core: 2. Of those that a mesh axis runs over, the one named last changes fastest.
Arguments:
- pair_rep: bfloat16 [128, 2048, 128], P('row', 'col'), may hold values from -6 to 6
- w_proj: bfloat16 [128, 512], replicated, may hold values from -0.5 to 0.5
- bias_logits: bfloat16 [4, 2048, 2048], P(None, 'row', 'col'), may hold values from -6 to 400
- chain_lengths: int32 [4], replicated, may hold values from 1 to 512, 1536 in all
- w_out: bfloat16 [128, 128], replicated, may hold values from -0.5 to 0.5
- grad_out: bfloat16 [128, 2048, 128], P('row', 'col'), may hold values from -96 to 96
Outputs:
- pair_grad: bfloat16 [128, 2048, 128], P('row', 'col')
- bias_grad: float32 [4, 2048, 2048], P(None, 'row', 'col')
- proj_grad: float32 [128, 512], replicated
- out_grad: float32 [128, 128], replicated
The draws below stay inside these ranges and needn't reach their ends.
All inputs are finite; a program needn't handle non-finite values.
Results may differ from the reference program's by a relative error of at most 0.015.
Values may be sent and summed in bfloat16 or wider, within the bound.
No kernel may reach another device: no remote copies, remote signals or barrier semaphores. Data moves between devices by JAX's collectives and lax.ppermute only.
A program may use at most 128 MiB of HBM per device.

```python
import math
import jax
import jax.numpy as jnp
import numpy as np
from jax import lax

C = 128
H = 4
D = 32
CHAINS = 4
I = 128
L = 2048


def draw_bias_logits(key, part):
    key = jax.random.fold_in(key, 11)
    key_base = jax.random.fold_in(key, 0)
    base_vals = jnp.clip(jax.random.normal(key_base, (H, L, L), jnp.float32), -6.0, 6.0)
    return base_vals.astype(jnp.bfloat16)


def steps_of(stream_key, extent, cuts, low, largest):
    def one(axis_at, shards_of):
        draws = jax.random.uniform(jax.random.fold_in(jax.random.fold_in(stream_key, 6), axis_at), (shards_of,), jnp.float32, low / len(cuts), largest / len(cuts))
        return jnp.repeat(jnp.exp(draws), extent[axis_at] // shards_of).reshape((-1,) + (1,) * (len(extent) - axis_at - 1))

    factor_of = one(*cuts[0])
    for cut in cuts[1:]:
        factor_of = factor_of * one(*cut)
    return factor_of


def profile(amount, total, most, lean):
    loads = [(1 << 20) // math.isqrt(standing ** lean) + 1 for standing in range(2, amount + 1)]
    surplus, given = total - most - (amount - 1), [1] * (amount - 1)
    while surplus > 0:
        free = [i for i in range(amount - 1) if given[i] < most]
        mass, left = sum([loads[i] for i in free]), surplus
        for i in free:
            more = min(most - given[i], max(1, left * loads[i] // mass), surplus)
            given[i] = given[i] + more
            surplus = surplus - more
    return np.array([most] + given)


def uneven(stream_key, count, total, limit, lean):
    if count == 2:
        one = jax.random.randint(stream_key, (), max(1, total - limit), min(limit, total - 1) + 1)
        return jnp.stack([one, total - one])
    lengths = jnp.asarray(profile(count, total, limit, lean), jnp.int32)
    pairs = (count - 1) // 2
    source_of, taker = lengths[1:1 + 2 * pairs:2], lengths[2:2 + 2 * pairs:2]
    room = jnp.minimum(source_of - 1, limit - taker)
    passed = jax.random.randint(jax.random.fold_in(stream_key, 1), (pairs,), 0, 1 << 20) % (room + 1)
    lengths = lengths.at[1:1 + 2 * pairs:2].set(source_of - passed).at[2:2 + 2 * pairs:2].set(taker + passed)
    return lengths[jax.random.permutation(jax.random.fold_in(stream_key, 2), count)]


def gaussian(rng, dims, width, bound, cuts=(), held_as=jnp.bfloat16):
    loudness = steps_of(rng, dims, cuts, -0.22, 0.18) if cuts else 1.0
    result = jax.random.normal(rng, dims, jnp.float32) * width * loudness
    return jnp.minimum(jnp.maximum(result, -bound), bound).astype(held_as)


def setup_inputs(seed: int = 0) -> dict:
    streams_of = jax.random.split(jax.random.key(seed), 7)
    pair_rep = gaussian(streams_of[0], (I, L, C), 1.0, 6.0, ((0, 8), (1, 32)))
    w_proj = gaussian(streams_of[1], (C, 4 * H * D), C ** -0.5, 0.5)
    bias_logits = draw_bias_logits(jax.random.fold_in(streams_of[6], 71), 0)
    chain_lengths = uneven(streams_of[3], CHAINS, 3 * L // 4, L // CHAINS, 0).astype(jnp.int32)
    w_out = gaussian(streams_of[4], (H * D, C), (H * D) ** -0.5, 0.5)
    grad_out = gaussian(streams_of[5], (I, L, C), 16.0, 96.0, ((0, 8), (1, 32)))
    return {"pair_rep": pair_rep, "w_proj": w_proj, "bias_logits": bias_logits, "chain_lengths": chain_lengths, "w_out": w_out, "grad_out": grad_out}


NEG_BIG = -1e30


def key_valid(chain_lengths, length_total):
    slot_count = length_total // CHAINS
    position = jnp.arange(length_total, dtype=jnp.int32)
    chain_of = position // slot_count
    chain_ids = jnp.arange(CHAINS, dtype=jnp.int32)
    chain_limit = jnp.sum(jnp.where(chain_of[:, None] == chain_ids[None, :], chain_lengths[None, :], 0), axis=1)
    return (position % slot_count) < chain_limit


def reference(pair_rep, w_proj, bias_logits, chain_lengths, w_out, grad_out):
    score_scale = D ** -0.5
    key_mask = key_valid(chain_lengths, L)
    projected = jnp.dot(pair_rep, w_proj, preferred_element_type=jnp.float32).astype(jnp.bfloat16)
    out_heads_grad = jnp.dot(grad_out, w_out.T, preferred_element_type=jnp.float32).astype(jnp.bfloat16)
    bias_float = bias_logits.astype(jnp.float32)

    def one_row(bias_acc, inputs):
        proj_row, ograd_row = inputs
        head_parts = proj_row.reshape(L, H, 4, D).astype(jnp.float32)
        queries = head_parts[:, :, 0]
        keys_row = head_parts[:, :, 1]
        values_row = head_parts[:, :, 2]
        gates_row = head_parts[:, :, 3]
        scores = jnp.einsum("jhd,khd->hjk", queries, keys_row) * score_scale + bias_float
        scores = jnp.where(key_mask[None, None, :], scores, NEG_BIG)
        row_max = jnp.max(scores, axis=2, keepdims=True)
        exp_scores = jnp.exp(scores - row_max)
        attn_prob = exp_scores / jnp.sum(exp_scores, axis=2, keepdims=True)
        prob_half = lax.optimization_barrier(attn_prob.astype(jnp.bfloat16)).astype(jnp.float32)
        attended = jnp.einsum("hjk,khd->jhd", prob_half, values_row)
        gate_sig = jax.nn.sigmoid(gates_row)
        gated = (gate_sig * attended).astype(jnp.bfloat16)
        ograd = ograd_row.reshape(L, H, D).astype(jnp.float32)
        attn_grad = lax.optimization_barrier((ograd * gate_sig).astype(jnp.bfloat16)).astype(jnp.float32)
        gate_grad = ograd * attended * gate_sig * (1.0 - gate_sig)
        value_grad = jnp.einsum("hjk,jhd->khd", prob_half, attn_grad)
        prob_grad = jnp.einsum("jhd,khd->hjk", attn_grad, values_row)
        delta_row = jnp.sum(attn_grad * attended, axis=2)
        score_grad = attn_prob * (prob_grad - delta_row.T[:, :, None])
        score_half = lax.optimization_barrier(score_grad.astype(jnp.bfloat16)).astype(jnp.float32)
        query_grad = jnp.einsum("hjk,khd->jhd", score_half, keys_row) * score_scale
        key_grad = jnp.einsum("hjk,jhd->khd", score_half, queries) * score_scale
        proj_row_grad = jnp.stack([query_grad, key_grad, value_grad, gate_grad], axis=2)
        proj_row_grad = proj_row_grad.reshape(L, 4 * H * D).astype(jnp.bfloat16)
        return bias_acc + score_grad, (proj_row_grad, gated.reshape(L, H * D))

    bias_grad, (proj_grads, gated_all) = lax.scan(one_row, jnp.zeros((H, L, L), jnp.float32), (projected, out_heads_grad))
    pair_grad = jnp.dot(proj_grads, w_proj.T, preferred_element_type=jnp.float32).astype(jnp.bfloat16)
    proj_grad = jnp.dot(pair_rep.reshape(-1, C).T, proj_grads.reshape(-1, 4 * H * D), preferred_element_type=jnp.float32) / L
    out_grad = jnp.dot(gated_all.reshape(-1, H * D).T, grad_out.reshape(-1, C), preferred_element_type=jnp.float32) / L
    return (pair_grad, bias_grad, proj_grad, out_grad)
```

```python
import jax
import jax.numpy as jnp
import numpy as np
from jax import lax
from jax.experimental import pallas as pl
from jax.experimental.pallas import tpu as pltpu
from jax.sharding import Mesh
from jax.sharding import PartitionSpec as P

H = 4
D = 32
CHAINS = 4
NEG_BIG = -1e30
LOG2E = 1.4426950408889634
SCALE = D ** (-0.5)
F32 = jnp.float32
BF16 = jnp.bfloat16
QUAD = 4
TOK = 64
SUB = 16
COLS = 32
ROWS = 8
LEN = TOK * COLS
QRY = SUB * COLS
VMEM_LIMIT = 56 * 1024 * 1024


def dot(a, b, dims):
    return lax.dot_general(a, b, (dims, ((), ())), preferred_element_type=F32)


def nn(a, b):
    return dot(a, b, ((1,), (0,)))


def nt(a, b):
    return dot(a, b, ((1,), (1,)))


def tn(a, b):
    return dot(a, b, ((0,), (0,)))


def lane_group(shape):
    return (lax.broadcasted_iota(jnp.int32, shape, 1) // D) % QUAD


def swap_halves(x):
    return jnp.concatenate([x[:, TOK:], x[:, :TOK]], axis=1)


def bias_pack_kernel(limit_ref, perm_ref, bias_ref, out_ref):
    low = lax.broadcasted_iota(jnp.int32, (32, 128), 1) < 64
    valid = lax.broadcasted_iota(jnp.int32, (TOK, 256), 0) < limit_ref[0]
    for h in range(H):
        turned = tn(bias_ref[h], perm_ref[...])
        turned = jnp.where(valid, turned, NEG_BIG)
        for m in range(2):
            top = turned[:32, m * 128 : (m + 1) * 128]
            bottom = turned[32:, m * 128 : (m + 1) * 128]
            out_ref[h * 4 + 2 * m] = jnp.where(low, top, swap_halves(bottom)).astype(BF16)
            out_ref[h * 4 + 2 * m + 1] = jnp.where(low, swap_halves(top), bottom).astype(BF16)


def bias_unpack_kernel(perm_ref, parts_ref, out_ref):
    low = lax.broadcasted_iota(jnp.int32, (32, 128), 1) < 64
    for h in range(H):
        tops, bottoms = [], []
        for m in range(2):
            first = parts_ref[h * 4 + 2 * m].astype(F32)
            second = parts_ref[h * 4 + 2 * m + 1].astype(F32)
            tops.append(jnp.where(low, first, swap_halves(second)))
            bottoms.append(jnp.where(low, swap_halves(first), second))
        whole = jnp.concatenate(
            [jnp.concatenate(tops, axis=1), jnp.concatenate(bottoms, axis=1)], axis=0
        ).astype(BF16)
        out_ref[h] = nt(perm_ref[...], whole)


def project_kernel(pair_ref, grad_ref, wp_ref, wo_ref, send_ref, gates_ref, ograd_ref):
    wp = wp_ref[...]
    wo = wo_ref[...]
    group_p = lane_group(wp.shape)
    group_o = lane_group(wo.shape)
    zero = jnp.zeros((), BF16)
    wide_p = jnp.concatenate([jnp.where(group_p == r, wp, zero) for r in range(QUAD)], axis=0)
    wide_o = jnp.concatenate([jnp.where(group_o == r, wo, zero) for r in range(QUAD)], axis=0)

    def quads(ref):
        return jnp.concatenate(
            [
                jnp.concatenate([ref[4 * q + r] for r in range(QUAD)], axis=1)
                for q in range(4)
            ],
            axis=0,
        )

    proj = nn(quads(pair_ref), wide_p).astype(BF16)
    ograd = nn(quads(grad_ref), wide_o).astype(BF16)
    for q in range(4):
        rows = slice(q * TOK, (q + 1) * TOK)
        qq = q % 2
        for h in range(H):
            query, key, value, gate = [
                proj[rows, h * 512 + p * 128 : h * 512 + (p + 1) * 128] for p in range(4)
            ]
            og = ograd[rows, h * 128 : (h + 1) * 128]
            gates_ref[q, :, h * 128 : (h + 1) * 128] = gate
            ograd_ref[q, :, h * 128 : (h + 1) * 128] = og
            cot = (og.astype(F32) * jax.nn.sigmoid(gate.astype(F32))).astype(BF16)
            for j in range(4):
                dest = (q // 2) * 16 + h * 4 + j
                send_ref[dest, qq * TOK : (qq + 1) * TOK] = value if j % 2 else key
                part = slice(j * SUB, (j + 1) * SUB)
                send_ref[dest, 128 + qq * SUB : 128 + (qq + 1) * SUB] = query[part]
                send_ref[dest, 160 + qq * SUB : 160 + (qq + 1) * SUB] = cot[part]


CHUNK = 256


def attend_kernel(
    core_ref,
    recv_ref,
    other_ref,
    bias_ref,
    kv_out,
    qo_out,
    bg_out,
    b32,
    s_ref,
    acc,
    kq,
    vq,
    kqt,
    vqt,
    dk,
    dv,
):
    core = core_ref[0]
    low = lax.broadcasted_iota(jnp.int32, (32, 128), 1) < 64

    def build(n, _):
        yl, blk = n // 16, n % 16
        at = pl.multiple_of(n * 64, 64)
        for m in range(4):
            left = bias_ref[4 * m + yl, blk].astype(F32) * LOG2E
            right = bias_ref[4 * m + 2 + yl, blk].astype(F32) * LOG2E
            lanes = slice(m * 128, (m + 1) * 128)
            b32[pl.ds(at, 32), lanes] = jnp.where(low, left, swap_halves(right))
            b32[pl.ds(at + 32, 32), lanes] = jnp.where(low, swap_halves(left), right)
        return 0

    lax.fori_loop(0, 32, build, 0)
    acc[...] = jnp.zeros_like(acc)
    steps = LEN // CHUNK

    def quad(q, _):
        at = pl.multiple_of(q * TOK, TOK)
        mine = recv_ref[:, pl.ds(at, TOK), :].reshape(LEN, 128)
        theirs = other_ref[:, pl.ds(at, TOK), :].reshape(LEN, 128)
        keys = jnp.where(core == 0, mine, theirs)
        values = jnp.where(core == 0, theirs, mine)
        kq[...] = keys
        vq[...] = values
        kqt[...] = keys.T
        vqt[...] = values.T
        sub = pl.multiple_of(q * SUB, SUB)
        query = recv_ref[:, pl.ds(128 + sub, SUB), :].reshape(QRY, 128)
        cot = recv_ref[:, pl.ds(160 + sub, SUB), :].reshape(QRY, 128)
        query_t = query.T
        cot_t = cot.T
        dk[...] = jnp.zeros_like(dk)
        dv[...] = jnp.zeros_like(dv)
        lanes = lane_group((QRY, 128))
        subs = lax.broadcasted_iota(jnp.int32, (128, QRY), 0) // D
        zero = jnp.zeros((), BF16)
        out_t, dq_t = [], []
        for i in range(QUAD):
            band = slice(i * D, (i + 1) * D)
            q_m = jnp.where(lanes == i, query, zero)
            c_m = jnp.where(lanes == i, cot, zero)
            qt_m = jnp.where(subs == i, query_t, zero)
            ct_m = jnp.where(subs == i, cot_t, zero)

            def score(c, top, qt_m=qt_m):
                rows = pl.ds(pl.multiple_of(c * CHUNK, CHUNK), CHUNK)
                s = nn(kq[rows, :], qt_m) * (SCALE * LOG2E) + b32[rows, :]
                s_ref[rows, :] = s
                return jnp.maximum(top, jnp.max(s.reshape(CHUNK // 8, 8, QRY), axis=0))

            top = lax.fori_loop(0, steps, score, jnp.full((8, QRY), -3e38, F32), unroll=2)
            top = jnp.max(top, axis=0, keepdims=True)

            def weigh(c, carry, band=band, top=top):
                total, out = carry
                rows = pl.ds(pl.multiple_of(c * CHUNK, CHUNK), CHUNK)
                e = jnp.exp2(s_ref[rows, :] - top)
                s_ref[rows, :] = e
                total = total + jnp.sum(e.reshape(CHUNK // 8, 8, QRY), axis=0)
                out = out + nn(vqt[band, rows], e.astype(BF16))
                return total, out

            total, out = lax.fori_loop(
                0,
                steps,
                weigh,
                (jnp.zeros((8, QRY), F32), jnp.zeros((D, QRY), F32)),
                unroll=2,
            )
            inv = 1.0 / jnp.sum(total, axis=0, keepdims=True)
            out = out * inv
            delta = jnp.sum(cot_t[band].astype(F32) * out, axis=0, keepdims=True)

            def back(c, dq, band=band, inv=inv, delta=delta, q_m=q_m, c_m=c_m, ct_m=ct_m):
                rows = pl.ds(pl.multiple_of(c * CHUNK, CHUNK), CHUNK)
                prob = s_ref[rows, :] * inv
                ds = prob * (nn(vq[rows, :], ct_m) - delta)
                acc[rows, :] += ds
                half = ds.astype(BF16)
                dk[rows, :] += nn(half, q_m)
                dv[rows, :] += nn(prob.astype(BF16), c_m)
                return dq + nn(kqt[band, rows], half)

            dq = lax.fori_loop(0, steps, back, jnp.zeros((D, QRY), F32), unroll=2)
            out_t.append(out)
            dq_t.append(dq * SCALE)
        qo_out[:, pl.ds(sub, SUB), :] = (
            jnp.concatenate(dq_t, axis=0).T.astype(BF16).reshape(COLS, SUB, 128)
        )
        qo_out[:, pl.ds(32 + sub, SUB), :] = (
            jnp.concatenate(out_t, axis=0).T.astype(BF16).reshape(COLS, SUB, 128)
        )
        kv_out[core, :, pl.ds(at, TOK), :] = (
            (dk[...] * SCALE).astype(BF16).reshape(COLS, TOK, 128)
        )
        kv_out[1 - core, :, pl.ds(at, TOK), :] = dv[...].astype(BF16).reshape(COLS, TOK, 128)
        return 0

    lax.fori_loop(0, 2, quad, 0)

    def spread(n, _):
        yl, blk = n // 16, n % 16
        at = pl.multiple_of(n * 64, 64)
        for m in range(4):
            lanes = slice(m * 128, (m + 1) * 128)
            top = acc[pl.ds(at, 32), lanes]
            bottom = acc[pl.ds(at + 32, 32), lanes]
            bg_out[4 * m + yl, blk] = jnp.where(low, top, swap_halves(bottom)).astype(BF16)
            bg_out[4 * m + 2 + yl, blk] = jnp.where(low, swap_halves(top), bottom).astype(BF16)
        return 0

    lax.fori_loop(0, 32, spread, 0)


def finish_kernel(
    recv_ref, gates_ref, ograd_ref, pair_ref, grad_ref, wp_ref, pair_out, weight_out, pg, gt
):
    for q in range(4):
        rows = slice(q * TOK, (q + 1) * TOK)
        qq = q % 2
        wide = slice(qq * TOK, (qq + 1) * TOK)
        for h in range(H):
            base = (q // 2) * 16 + h * 4
            key = recv_ref[base, wide].astype(F32) + recv_ref[base + 2, wide].astype(F32)
            value = recv_ref[base + 1, wide].astype(F32) + recv_ref[base + 3, wide].astype(F32)
            query = jnp.concatenate(
                [recv_ref[base + j, 128 + qq * SUB : 128 + (qq + 1) * SUB] for j in range(4)],
                axis=0,
            )
            out = jnp.concatenate(
                [recv_ref[base + j, 160 + qq * SUB : 160 + (qq + 1) * SUB] for j in range(4)],
                axis=0,
            ).astype(F32)
            lanes = slice(h * 128, (h + 1) * 128)
            sig = jax.nn.sigmoid(gates_ref[q, :, lanes].astype(F32))
            og = ograd_ref[q, :, lanes].astype(F32)
            gt[rows, lanes] = (sig * out).astype(BF16)
            pg[rows, h * 512 : h * 512 + 128] = query
            pg[rows, h * 512 + 128 : h * 512 + 256] = key.astype(BF16)
            pg[rows, h * 512 + 256 : h * 512 + 384] = value.astype(BF16)
            pg[rows, h * 512 + 384 : h * 512 + 512] = (og * out * sig * (1.0 - sig)).astype(BF16)
    wp = wp_ref[...]
    group = lane_group(wp.shape)
    zero = jnp.zeros((), BF16)
    grads = pg[...]
    gated = gt[...]
    for r in range(QUAD):
        part = nt(grads, jnp.where(group == r, wp, zero)).astype(BF16)
        for q in range(4):
            pair_out[4 * q + r] = part[q * TOK : (q + 1) * TOK]
    turned = grads.T
    gated_t = gated.T
    for r in range(QUAD):
        pair_r = jnp.concatenate([pair_ref[4 * q + r] for q in range(4)], axis=0)
        grad_r = jnp.concatenate([grad_ref[4 * q + r] for q in range(4)], axis=0)
        for n in range(16):
            at = n * 128 + r * D
            piece = nn(turned[at : at + D], pair_r) * (1.0 / LEN)
            if r == 0:
                weight_out[n * D : (n + 1) * D] = piece
            else:
                weight_out[n * D : (n + 1) * D] += piece
        for n in range(4):
            at = n * 128 + r * D
            piece = nn(gated_t[at : at + D], grad_r) * (1.0 / LEN)
            where = slice(512 + n * D, 512 + (n + 1) * D)
            if r == 0:
                weight_out[where] = piece
            else:
                weight_out[where] += piece


def whole():
    return pl.BlockSpec(memory_space=pltpu.VMEM)


def scalar():
    return pl.BlockSpec(memory_space=pltpu.SMEM)


def call(kernel, in_specs, outs, scratch=(), flops=0, moved=0):
    return pl.pallas_call(
        kernel,
        out_shape=outs,
        in_specs=in_specs,
        out_specs=jax.tree.map(lambda _: whole(), outs),
        scratch_shapes=list(scratch),
        compiler_params=pltpu.CompilerParams(vmem_limit_bytes=VMEM_LIMIT),
        cost_estimate=pl.CostEstimate(flops=flops, bytes_accessed=moved, transcendentals=0),
    )


def shape(dims, dtype=BF16):
    return jax.ShapeDtypeStruct(dims, dtype)


def query_order():
    perm = np.zeros((256, 256), np.float32)
    for s in range(4):
        for j in range(4):
            for t in range(SUB):
                perm[s * 64 + j * SUB + t, j * 64 + s * SUB + t] = 1.0
    return perm


def widen(groups):
    source = lax.broadcasted_iota(jnp.int32, (groups * D, groups * 128), 0)
    target = lax.broadcasted_iota(jnp.int32, (groups * D, groups * 128), 1)
    same = (source // D == target // 128) & (source % D == target % D)
    return same.astype(BF16)


def on_device(pair_rep, w_proj, bias_logits, chain_lengths, w_out, grad_out):
    block = lax.axis_index(("yl", "z", "c"))
    core = lax.axis_index("c")
    col = ("yl", "z", "c")
    plane = ("yh", "x", "yl")
    per_chain = COLS // CHAINS
    chain = lax.dynamic_index_in_dim(chain_lengths, block // per_chain, 0, keepdims=True)
    limit = chain - (block % per_chain) * TOK
    perm = jnp.asarray(query_order(), BF16)

    packed = call(bias_pack_kernel, [scalar(), whole(), whole()], shape((16, 32, 128)))(
        limit, perm, bias_logits
    )
    bias_z = lax.all_to_all(packed, ("z", "c"), 0, 0, tiled=True)
    bias_all = lax.all_to_all(
        jnp.broadcast_to(bias_z[None], (16, 16, 32, 128)), plane, 0, 0, tiled=True
    )

    wp = jnp.dot(w_proj, widen(16), preferred_element_type=F32).astype(BF16)
    wo = jnp.dot(w_out.T, widen(4), preferred_element_type=F32).astype(BF16)
    send, gates, ograd = call(
        project_kernel,
        [whole()] * 4,
        (shape((COLS, 192, 128)), shape((4, TOK, 512)), shape((4, TOK, 512))),
        flops=700_000_000,
        moved=6_000_000,
    )(pair_rep, grad_out, wp, wo)
    recv = lax.all_to_all(send, col, 0, 0, tiled=True)
    other = lax.ppermute(recv[:, :128], "c", [(0, 1), (1, 0)])
    kv, qo, bg = call(
        attend_kernel,
        [scalar(), whole(), whole(), whole()],
        (shape((2, COLS, 128, 128)), shape((COLS, 64, 128)), shape((16, 16, 32, 128))),
        [
            pltpu.VMEM((LEN, QRY), F32),
            pltpu.VMEM((LEN, QRY), F32),
            pltpu.VMEM((LEN, QRY), F32),
            pltpu.VMEM((LEN, 128), BF16),
            pltpu.VMEM((LEN, 128), BF16),
            pltpu.VMEM((128, LEN), BF16),
            pltpu.VMEM((128, LEN), BF16),
            pltpu.VMEM((LEN, 128), F32),
            pltpu.VMEM((LEN, 128), F32),
        ],
        flops=30_000_000_000,
        moved=10_000_000,
    )(core[None].astype(jnp.int32), recv, other, bias_all)
    given = lax.ppermute(kv[1], "c", [(0, 1), (1, 0)])
    kept = (kv[0].astype(F32) + given.astype(F32)).astype(BF16)
    home = lax.all_to_all(jnp.concatenate([kept, qo], axis=1), col, 0, 0, tiled=True)
    bg_parts = lax.all_to_all(bg, plane, 0, 0, tiled=True)
    bg_sum = jnp.sum(bg_parts.astype(F32), axis=0).astype(BF16)
    bg_home = lax.all_to_all(bg_sum, ("z", "c"), 0, 0, tiled=True)
    bias_grad = call(bias_unpack_kernel, [whole()] * 2, shape((H, 256, TOK), F32))(perm, bg_home)
    pair_grad, weights = call(
        finish_kernel,
        [whole()] * 6,
        (shape((16, TOK, 128)), shape((640, 128), F32)),
        [pltpu.VMEM((256, 2048), BF16), pltpu.VMEM((256, 512), BF16)],
        flops=1_000_000_000,
        moved=4_000_000,
    )(home, gates, ograd, pair_rep, grad_out, wp)
    every = ("yh", "x", "yl", "z", "c")
    pieces = jnp.pad(weights, ((0, 128), (0, 0))).reshape(256, 3, 128)
    summed = jnp.sum(lax.all_to_all(pieces, every, 0, 0, tiled=True), axis=0)
    total = lax.all_to_all(
        jnp.broadcast_to(summed[None], (256, 3, 128)), every, 0, 0, tiled=True
    ).reshape(768, 128)
    return (pair_grad, bias_grad, total[:512].T, total[512:640])


def solution(mesh):
    fine = Mesh(mesh.devices.reshape(2, 4, 2, 8, 2), ("yh", "x", "yl", "z", "c"))
    row = ("yh", "x")
    col = ("yl", "z", "c")
    return jax.shard_map(
        on_device,
        mesh=fine,
        in_specs=(
            P(row, col, None),
            P(),
            P(None, row, col),
            P(),
            P(),
            P(row, col, None),
        ),
        out_specs=(P(row, col, None), P(None, row, col), P(), P()),
        check_vma=False,
    )
```

```python
import jax
import jax.numpy as jnp
import numpy as np
from jax import lax
from jax.experimental import pallas as pl
from jax.experimental.pallas import tpu as pltpu
from jax.sharding import Mesh
from jax.sharding import PartitionSpec as P

H = 4
D = 32
CHAINS = 4
NEG_BIG = -1e30
LOG2E = 1.4426950408889634
SCALE = D ** (-0.5)
F32 = jnp.float32
BF16 = jnp.bfloat16
QUAD = 4
TOK = 64
SUB = 16
COLS = 32
ROWS = 8
LEN = TOK * COLS
QRY = SUB * COLS
VMEM_LIMIT = 56 * 1024 * 1024


def dot(a, b, dims):
    return lax.dot_general(a, b, (dims, ((), ())), preferred_element_type=F32)


def nn(a, b):
    return dot(a, b, ((1,), (0,)))


def nt(a, b):
    return dot(a, b, ((1,), (1,)))


def tn(a, b):
    return dot(a, b, ((0,), (0,)))


def lane_group(shape):
    return (lax.broadcasted_iota(jnp.int32, shape, 1) // D) % QUAD


def swap_halves(x):
    return jnp.concatenate([x[:, TOK:], x[:, :TOK]], axis=1)


def bias_pack_kernel(limit_ref, perm_ref, bias_ref, out_ref):
    z, core = limit_ref[1], limit_ref[2]
    low = lax.broadcasted_iota(jnp.int32, (32, 128), 1) < 64
    valid = lax.broadcasted_iota(jnp.int32, (TOK, 256), 0) < limit_ref[0]
    for h in range(H):
        turned = tn(bias_ref[h], perm_ref[...])
        turned = jnp.where(valid, turned, NEG_BIG)
        for m in range(2):
            top = turned[:32, m * 128 : (m + 1) * 128]
            bottom = turned[32:, m * 128 : (m + 1) * 128]
            slot = z ^ (2 * h + m)
            out_ref[core, slot] = jnp.where(low, top, swap_halves(bottom)).astype(BF16)
            out_ref[1 - core, slot] = jnp.where(low, swap_halves(top), bottom).astype(BF16)


def bias_unpack_kernel(place_ref, perm_ref, parts_ref, given_ref, out_ref):
    z, core = place_ref[1], place_ref[2]
    low = lax.broadcasted_iota(jnp.int32, (32, 128), 1) < 64
    for h in range(H):
        tops, bottoms = [], []
        for m in range(2):
            slot = z ^ (2 * h + m)
            same = parts_ref[slot, 0].astype(F32)
            across = given_ref[slot].astype(F32)
            first = jnp.where(core == 0, same, across)
            second = jnp.where(core == 0, across, same)
            tops.append(jnp.where(low, first, swap_halves(second)))
            bottoms.append(jnp.where(low, swap_halves(first), second))
        whole = jnp.concatenate(
            [jnp.concatenate(tops, axis=1), jnp.concatenate(bottoms, axis=1)], axis=0
        ).astype(BF16)
        out_ref[h] = nt(perm_ref[...], whole)


def project_kernel(
    pair_ref, grad_ref, wp_ref, wo_ref, send_a_ref, send_b_ref, gates_ref, ograd_ref
):
    wp = wp_ref[...]
    wo = wo_ref[...]
    group_p = lane_group(wp.shape)
    group_o = lane_group(wo.shape)
    zero = jnp.zeros((), BF16)
    wide_p = jnp.concatenate([jnp.where(group_p == r, wp, zero) for r in range(QUAD)], axis=0)
    wide_o = jnp.concatenate([jnp.where(group_o == r, wo, zero) for r in range(QUAD)], axis=0)

    def quads(ref):
        return jnp.concatenate(
            [
                jnp.concatenate([ref[4 * q + r] for r in range(QUAD)], axis=1)
                for q in range(4)
            ],
            axis=0,
        )

    proj = nn(quads(pair_ref), wide_p).astype(BF16)
    ograd = nn(quads(grad_ref), wide_o).astype(BF16)
    for q in range(4):
        rows = slice(q * TOK, (q + 1) * TOK)
        send_ref = send_b_ref if q % 2 else send_a_ref
        for h in range(H):
            query, key, value, gate = [
                proj[rows, h * 512 + p * 128 : h * 512 + (p + 1) * 128] for p in range(4)
            ]
            og = ograd[rows, h * 128 : (h + 1) * 128]
            gates_ref[q, :, h * 128 : (h + 1) * 128] = gate
            ograd_ref[q, :, h * 128 : (h + 1) * 128] = og
            cot = (og.astype(F32) * jax.nn.sigmoid(gate.astype(F32))).astype(BF16)
            for j in range(4):
                dest = (q // 2) * 16 + h * 4 + j
                send_ref[dest, :TOK] = value if j % 2 else key
                part = slice(j * SUB, (j + 1) * SUB)
                send_ref[dest, TOK : TOK + SUB] = query[part]
                send_ref[dest, TOK + SUB :] = cot[part]


CHUNK = 256


def attend_kernel(first, place_ref, recv_ref, other_ref, *refs):
    bias_refs, refs = refs[:4], refs[4:]
    if first:
        kv_out, qo_out, acc, *refs = refs
    else:
        acc_in, kv_out, qo_out, *refs = refs
        bg_outs, (acc, *refs) = refs[:4], refs[4:]
    b32, s_ref, kq, vq, kqt, vqt, dk, dv = refs
    yh, x, yl, z, core = [place_ref[n] for n in range(5)]
    low = lax.broadcasted_iota(jnp.int32, (32, 128), 1) < 64

    def row_of(zs, cs, yls):
        return pl.multiple_of((((yl ^ yls) * 8 + (z ^ zs)) * 2 + (core ^ cs)) * TOK, TOK)

    def build(n, _):
        zs, cs = n // 2, n % 2
        for yls in range(2):
            at = row_of(zs, cs, yls)
            for m in range(4):
                ref = bias_refs[(m // 2) * 2 + yls]
                left = ref[2 * (m % 2), zs, cs].astype(F32) * LOG2E
                right = ref[2 * (m % 2) + 1, zs, cs].astype(F32) * LOG2E
                lanes = slice(m * 128, (m + 1) * 128)
                b32[pl.ds(at, 32), lanes] = jnp.where(low, left, swap_halves(right))
                b32[pl.ds(at + 32, 32), lanes] = jnp.where(low, swap_halves(left), right)
        return 0

    lax.fori_loop(0, 16, build, 0)
    acc[...] = jnp.zeros_like(acc) if first else acc_in[...]
    steps = LEN // CHUNK

    homes = [((yh ^ (p // 4)) * 4 + (x ^ (p % 4))) * 4 for p in range(ROWS)]

    def queries(lo):
        return jnp.concatenate(
            [recv_ref[pl.ds(at, 4), lo : lo + SUB, :].reshape(TOK, 128) for at in homes], axis=0
        )

    mine = recv_ref[:, :TOK, :].reshape(LEN, 128)
    theirs = other_ref[...].reshape(LEN, 128)
    keys = jnp.where(core == 0, mine, theirs)
    values = jnp.where(core == 0, theirs, mine)
    kq[...] = keys
    vq[...] = values
    kqt[...] = keys.T
    vqt[...] = values.T
    query = queries(TOK)
    cot = queries(TOK + SUB)
    query_t = query.T
    cot_t = cot.T
    dk[...] = jnp.zeros_like(dk)
    dv[...] = jnp.zeros_like(dv)
    lanes = lane_group((QRY, 128))
    subs = lax.broadcasted_iota(jnp.int32, (128, QRY), 0) // D
    zero = jnp.zeros((), BF16)
    out_t, dq_t = [], []
    for i in range(QUAD):
        band = slice(i * D, (i + 1) * D)
        q_m = jnp.where(lanes == i, query, zero)
        c_m = jnp.where(lanes == i, cot, zero)
        qt_m = jnp.where(subs == i, query_t, zero)
        ct_m = jnp.where(subs == i, cot_t, zero)

        def score(c, top, qt_m=qt_m):
            rows = pl.ds(pl.multiple_of(c * CHUNK, CHUNK), CHUNK)
            s = nn(kq[rows, :], qt_m) * (SCALE * LOG2E) + b32[rows, :]
            s_ref[rows, :] = s
            return jnp.maximum(top, jnp.max(s.reshape(CHUNK // 8, 8, QRY), axis=0))

        top = lax.fori_loop(0, steps, score, jnp.full((8, QRY), -3e38, F32), unroll=2)
        top = jnp.max(top, axis=0, keepdims=True)

        def weigh(c, carry, band=band, top=top):
            total, out = carry
            rows = pl.ds(pl.multiple_of(c * CHUNK, CHUNK), CHUNK)
            e = jnp.exp2(s_ref[rows, :] - top)
            s_ref[rows, :] = e
            total = total + jnp.sum(e.reshape(CHUNK // 8, 8, QRY), axis=0)
            out = out + nn(vqt[band, rows], e.astype(BF16))
            return total, out

        total, out = lax.fori_loop(
            0,
            steps,
            weigh,
            (jnp.zeros((8, QRY), F32), jnp.zeros((D, QRY), F32)),
            unroll=2,
        )
        inv = 1.0 / jnp.sum(total, axis=0, keepdims=True)
        out = out * inv
        delta = jnp.sum(cot_t[band].astype(F32) * out, axis=0, keepdims=True)

        def back(c, dq, band=band, inv=inv, delta=delta, q_m=q_m, c_m=c_m, ct_m=ct_m):
            rows = pl.ds(pl.multiple_of(c * CHUNK, CHUNK), CHUNK)
            prob = s_ref[rows, :] * inv
            ds = prob * (nn(vq[rows, :], ct_m) - delta)
            acc[rows, :] += ds
            half = ds.astype(BF16)
            dk[rows, :] += nn(half, q_m)
            dv[rows, :] += nn(prob.astype(BF16), c_m)
            return dq + nn(kqt[band, rows], half)

        dq = lax.fori_loop(0, steps, back, jnp.zeros((D, QRY), F32), unroll=2)
        out_t.append(out)
        dq_t.append(dq * SCALE)
    dq = jnp.concatenate(dq_t, axis=0).T.astype(BF16)
    out = jnp.concatenate(out_t, axis=0).T.astype(BF16)
    for p, at in enumerate(homes):
        part = slice(p * TOK, (p + 1) * TOK)
        qo_out[pl.ds(at, 4), :SUB, :] = dq[part].reshape(4, SUB, 128)
        qo_out[pl.ds(at, 4), SUB:, :] = out[part].reshape(4, SUB, 128)
    kv_out[core] = (dk[...] * SCALE).astype(BF16).reshape(COLS, TOK, 128)
    kv_out[1 - core] = dv[...].astype(BF16).reshape(COLS, TOK, 128)
    if first:
        return

    def spread(n, _):
        zs, cs = n // 2, n % 2
        for yls in range(2):
            at = row_of(zs, cs, yls)
            for m in range(4):
                ref = bg_outs[(m // 2) * 2 + yls]
                lanes = slice(m * 128, (m + 1) * 128)
                top = acc[pl.ds(at, 32), lanes]
                bottom = acc[pl.ds(at + 32, 32), lanes]
                left = jnp.where(low, top, swap_halves(bottom))
                right = jnp.where(low, swap_halves(top), bottom)
                ref[2 * (m % 2), zs, cs] = left.astype(BF16)
                ref[2 * (m % 2) + 1, zs, cs] = right.astype(BF16)
        return 0

    lax.fori_loop(0, 16, spread, 0)


def finish_kernel(
    recv_a_ref,
    recv_b_ref,
    gates_ref,
    ograd_ref,
    pair_ref,
    grad_ref,
    wp_ref,
    pair_out,
    weight_out,
    pg,
    gt,
):
    for q in range(4):
        rows = slice(q * TOK, (q + 1) * TOK)
        recv_ref = recv_b_ref if q % 2 else recv_a_ref
        wide = slice(0, TOK)
        for h in range(H):
            base = (q // 2) * 16 + h * 4
            key = recv_ref[base, wide].astype(F32) + recv_ref[base + 2, wide].astype(F32)
            value = recv_ref[base + 1, wide].astype(F32) + recv_ref[base + 3, wide].astype(F32)
            query = jnp.concatenate(
                [recv_ref[base + j, TOK : TOK + SUB] for j in range(4)],
                axis=0,
            )
            out = jnp.concatenate(
                [recv_ref[base + j, TOK + SUB :] for j in range(4)],
                axis=0,
            ).astype(F32)
            lanes = slice(h * 128, (h + 1) * 128)
            sig = jax.nn.sigmoid(gates_ref[q, :, lanes].astype(F32))
            og = ograd_ref[q, :, lanes].astype(F32)
            gt[rows, lanes] = (sig * out).astype(BF16)
            pg[rows, h * 512 : h * 512 + 128] = query
            pg[rows, h * 512 + 128 : h * 512 + 256] = key.astype(BF16)
            pg[rows, h * 512 + 256 : h * 512 + 384] = value.astype(BF16)
            pg[rows, h * 512 + 384 : h * 512 + 512] = (og * out * sig * (1.0 - sig)).astype(BF16)
    wp = wp_ref[...]
    group = lane_group(wp.shape)
    zero = jnp.zeros((), BF16)
    grads = pg[...]
    gated = gt[...]
    for r in range(QUAD):
        part = nt(grads, jnp.where(group == r, wp, zero)).astype(BF16)
        for q in range(4):
            pair_out[4 * q + r] = part[q * TOK : (q + 1) * TOK]
    turned = grads.T
    gated_t = gated.T
    for r in range(QUAD):
        pair_r = jnp.concatenate([pair_ref[4 * q + r] for q in range(4)], axis=0)
        grad_r = jnp.concatenate([grad_ref[4 * q + r] for q in range(4)], axis=0)
        for n in range(16):
            at = n * 128 + r * D
            piece = nn(turned[at : at + D], pair_r) * (1.0 / LEN)
            if r == 0:
                weight_out[n * D : (n + 1) * D] = piece
            else:
                weight_out[n * D : (n + 1) * D] += piece
        for n in range(4):
            at = n * 128 + r * D
            piece = nn(gated_t[at : at + D], grad_r) * (1.0 / LEN)
            where = slice(512 + n * D, 512 + (n + 1) * D)
            if r == 0:
                weight_out[where] = piece
            else:
                weight_out[where] += piece


def whole():
    return pl.BlockSpec(memory_space=pltpu.VMEM)


def scalar():
    return pl.BlockSpec(memory_space=pltpu.SMEM)


def call(kernel, in_specs, outs, scratch=(), flops=0, moved=0):
    return pl.pallas_call(
        kernel,
        out_shape=outs,
        in_specs=in_specs,
        out_specs=jax.tree.map(lambda _: whole(), outs),
        scratch_shapes=list(scratch),
        compiler_params=pltpu.CompilerParams(vmem_limit_bytes=VMEM_LIMIT),
        cost_estimate=pl.CostEstimate(flops=flops, bytes_accessed=moved, transcendentals=0),
    )


def shape(dims, dtype=BF16):
    return jax.ShapeDtypeStruct(dims, dtype)


def query_order():
    perm = np.zeros((256, 256), np.float32)
    for s in range(4):
        for j in range(4):
            for t in range(SUB):
                perm[s * 64 + j * SUB + t, j * 64 + s * SUB + t] = 1.0
    return perm


def widen(groups):
    source = lax.broadcasted_iota(jnp.int32, (groups * D, groups * 128), 0)
    target = lax.broadcasted_iota(jnp.int32, (groups * D, groups * 128), 1)
    same = (source // D == target // 128) & (source % D == target % D)
    return same.astype(BF16)


def flip(x, axes, bits):
    count = {"x": 4, "y": 4, "z": 8, "c": 2}[axes]
    names = ("yh", "yl") if axes == "y" else axes
    return lax.ppermute(x, names, [(n, n ^ bits) for n in range(count)])


PIECE = (32, 128)


def gather_bias(packed):
    across = flip(packed[1], "c", 1)
    both = jnp.stack([packed[0], across], axis=1)
    both = jnp.stack([both[0]] + [flip(both[s], "z", s) for s in range(1, 8)])
    line = jnp.stack([both] + [flip(both, "x", s) for s in range(1, 4)])
    return [line] + [flip(line, "y", s) for s in range(1, 4)]


def total(first, others):
    result = first.astype(F32)
    for other in others:
        result = result + other.astype(F32)
    return result.astype(BF16)


def scatter_bias(parts):
    line = total(parts[0], [flip(parts[s], "y", s) for s in range(1, 4)])
    both = total(line[0], [flip(line[s], "x", s) for s in range(1, 4)])
    both = jnp.stack([both[0]] + [flip(both[s], "z", s) for s in range(1, 8)])
    return both, flip(both[:, 1], "c", 1)


def attend(first, place, recv, bias, acc=()):
    other = flip(recv[:, :TOK], "c", 1)
    big = (LEN, QRY)
    scratch = [pltpu.VMEM(big, F32), pltpu.VMEM(big, F32)]
    scratch += [pltpu.VMEM((LEN, 128), BF16)] * 2 + [pltpu.VMEM((128, LEN), BF16)] * 2
    scratch += [pltpu.VMEM((LEN, 128), F32)] * 2
    outs = (shape((2, COLS, TOK, 128)), shape((COLS, 2 * SUB, 128)))
    if first:
        outs += (shape(big, F32),)
    else:
        outs += (shape((4, 8, 2) + PIECE),) * 4
        scratch = [pltpu.VMEM(big, F32)] + scratch
    kv, qo, *rest = call(
        lambda *refs: attend_kernel(first, *refs),
        [scalar()] + [whole()] * (6 + len(acc)),
        outs,
        scratch,
        flops=25_000_000_000,
        moved=10_000_000,
    )(place, recv, other, *bias, *acc)
    kept = total(kv[0], [flip(kv[1], "c", 1)])
    return jnp.concatenate([kept, qo], axis=1), rest


def on_device(pair_rep, w_proj, bias_logits, chain_lengths, w_out, grad_out):
    block = lax.axis_index(("yl", "z", "c"))
    col = ("yl", "z", "c")
    per_chain = COLS // CHAINS
    chain = lax.dynamic_index_in_dim(chain_lengths, block // per_chain, 0, keepdims=False)
    limit = chain - (block % per_chain) * TOK
    place = jnp.stack([lax.axis_index(a) for a in ("yh", "x", "yl", "z", "c")]).astype(jnp.int32)
    perm = jnp.asarray(query_order(), BF16)

    packed = call(bias_pack_kernel, [scalar(), whole(), whole()], shape((2, 8) + PIECE))(
        jnp.stack([limit, place[3], place[4]]), perm, bias_logits
    )
    bias = gather_bias(packed)
    wp = jnp.dot(w_proj, widen(16), preferred_element_type=F32).astype(BF16)
    wo = jnp.dot(w_out.T, widen(4), preferred_element_type=F32).astype(BF16)
    part = shape((COLS, TOK + 2 * SUB, 128))
    send_a, send_b, gates, ograd = call(
        project_kernel,
        [whole()] * 4,
        (part, part, shape((4, TOK, 512)), shape((4, TOK, 512))),
        flops=700_000_000,
        moved=6_000_000,
    )(pair_rep, grad_out, wp, wo)
    recv_a = lax.all_to_all(send_a, col, 0, 0, tiled=True)
    recv_b = lax.all_to_all(send_b, col, 0, 0, tiled=True)
    back_a, acc = attend(True, place, recv_a, bias)
    home_a = lax.all_to_all(back_a, col, 0, 0, tiled=True)
    back_b, bg = attend(False, place, recv_b, bias, acc)
    home_b = lax.all_to_all(back_b, col, 0, 0, tiled=True)
    bias_grad = call(
        bias_unpack_kernel, [scalar()] + [whole()] * 3, shape((H, 256, TOK), F32)
    )(jnp.stack([limit, place[3], place[4]]), perm, *scatter_bias(bg))
    pair_grad, weights = call(
        finish_kernel,
        [whole()] * 7,
        (shape((16, TOK, 128)), shape((640, 128), F32)),
        [pltpu.VMEM((256, 2048), BF16), pltpu.VMEM((256, 512), BF16)],
        flops=1_000_000_000,
        moved=4_000_000,
    )(home_a, home_b, gates, ograd, pair_rep, grad_out, wp)
    every = ("yh", "x", "yl", "z", "c")
    pieces = jnp.pad(weights, ((0, 128), (0, 0))).reshape(256, 3, 128)
    summed = jnp.sum(lax.all_to_all(pieces, every, 0, 0, tiled=True), axis=0)
    whole_sum = lax.all_to_all(
        jnp.broadcast_to(summed[None], (256, 3, 128)), every, 0, 0, tiled=True
    ).reshape(768, 128)
    return (pair_grad, bias_grad, whole_sum[:512].T, whole_sum[512:640])


def solution(mesh):
    fine = Mesh(mesh.devices.reshape(2, 4, 2, 8, 2), ("yh", "x", "yl", "z", "c"))
    row = ("yh", "x")
    col = ("yl", "z", "c")
    return jax.shard_map(
        on_device,
        mesh=fine,
        in_specs=(
            P(row, col, None),
            P(),
            P(None, row, col),
            P(),
            P(),
            P(row, col, None),
        ),
        out_specs=(P(row, col, None), P(None, row, col), P(), P()),
        check_vma=False,
    )
```

```python
import jax
import jax.numpy as jnp
import numpy as np
from jax import lax
from jax.experimental import pallas as pl
from jax.experimental.pallas import tpu as pltpu
from jax.sharding import Mesh
from jax.sharding import PartitionSpec as P

H = 4
D = 32
CHAINS = 4
NEG_BIG = -1e30
LOG2E = 1.4426950408889634
SCALE = D ** (-0.5)
F32 = jnp.float32
BF16 = jnp.bfloat16
QUAD = 4
TOK = 64
SUB = 16
COLS = 32
ROWS = 8
LEN = TOK * COLS
QRY = SUB * COLS
VMEM_LIMIT = 56 * 1024 * 1024


def dot(a, b, dims):
    return lax.dot_general(a, b, (dims, ((), ())), preferred_element_type=F32)


def nn(a, b):
    return dot(a, b, ((1,), (0,)))


def nt(a, b):
    return dot(a, b, ((1,), (1,)))


def tn(a, b):
    return dot(a, b, ((0,), (0,)))


def lane_group(shape):
    return (lax.broadcasted_iota(jnp.int32, shape, 1) // D) % QUAD


def swap_halves(x):
    return jnp.concatenate([x[:, TOK:], x[:, :TOK]], axis=1)


def bias_pack_kernel(place_ref, chain_ref, perm_ref, bias_ref, out_ref):
    block = (place_ref[2] * 8 + place_ref[3]) * 2 + place_ref[4]
    per_chain = COLS // CHAINS
    limit = chain_ref[block // per_chain] - (block % per_chain) * TOK
    low = lax.broadcasted_iota(jnp.int32, (32, 128), 1) < 64
    valid = lax.broadcasted_iota(jnp.int32, (TOK, 256), 0) < limit
    for h in range(H):
        ordered = jnp.where(valid, nn(bias_ref[h], perm_ref[...]), NEG_BIG)
        for m in range(2):
            top = ordered[:32, m * 128 : (m + 1) * 128]
            bottom = ordered[32:, m * 128 : (m + 1) * 128]
            out_ref[h * 4 + 2 * m] = jnp.where(low, top, swap_halves(bottom)).astype(BF16)
            out_ref[h * 4 + 2 * m + 1] = jnp.where(low, swap_halves(top), bottom).astype(BF16)


def bias_unpack_kernel(perm_ref, parts_ref, out_ref):
    low = lax.broadcasted_iota(jnp.int32, (32, 128), 1) < 64
    for h in range(H):
        tops, bottoms = [], []
        for m in range(2):
            first = parts_ref[h * 4 + 2 * m, :32].astype(F32)
            second = parts_ref[h * 4 + 2 * m + 1, :32].astype(F32)
            tops.append(jnp.where(low, first, swap_halves(second)))
            bottoms.append(jnp.where(low, swap_halves(first), second))
        ordered = jnp.concatenate(
            [jnp.concatenate(tops, axis=1), jnp.concatenate(bottoms, axis=1)], axis=0
        ).astype(BF16)
        out_ref[h] = nt(ordered, perm_ref[...])


def project_kernel(
    pair_ref, grad_ref, wp_ref, wo_ref, send_a_ref, send_b_ref, gates_ref, ograd_ref
):
    wp = wp_ref[...]
    wo = wo_ref[...]
    group_p = lane_group(wp.shape)
    group_o = lane_group(wo.shape)
    zero = jnp.zeros((), BF16)
    wide_p = jnp.concatenate([jnp.where(group_p == r, wp, zero) for r in range(QUAD)], axis=0)
    wide_o = jnp.concatenate([jnp.where(group_o == r, wo, zero) for r in range(QUAD)], axis=0)

    def quads(ref):
        return jnp.concatenate(
            [
                jnp.concatenate([ref[4 * q + r] for r in range(QUAD)], axis=1)
                for q in range(4)
            ],
            axis=0,
        )

    proj = nn(quads(pair_ref), wide_p).astype(BF16)
    ograd = nn(quads(grad_ref), wide_o).astype(BF16)
    for q in range(4):
        rows = slice(q * TOK, (q + 1) * TOK)
        send_ref = send_b_ref if q % 2 else send_a_ref
        for h in range(H):
            query, key, value, gate = [
                proj[rows, h * 512 + p * 128 : h * 512 + (p + 1) * 128] for p in range(4)
            ]
            og = ograd[rows, h * 128 : (h + 1) * 128]
            gates_ref[q, :, h * 128 : (h + 1) * 128] = gate
            ograd_ref[q, :, h * 128 : (h + 1) * 128] = og
            cot = (og.astype(F32) * jax.nn.sigmoid(gate.astype(F32))).astype(BF16)
            for j in range(4):
                dest = (q // 2) * 16 + h * 4 + j
                send_ref[dest, :TOK] = value if j % 2 else key
                part = slice(j * SUB, (j + 1) * SUB)
                send_ref[dest, TOK : TOK + SUB] = query[part]
                send_ref[dest, TOK + SUB :] = cot[part]


CHUNK = 256


def attend_kernel(first, place_ref, recv_ref, other_ref, *refs):
    bias_refs, refs = refs[:8], refs[8:]
    if first:
        back_out, give_out, acc, *refs = refs
    else:
        acc_in, back_out, give_out, *refs = refs
        bg_outs, (acc, *refs) = refs[:8], refs[8:]
    b32, s_ref, kq, vq, kqt, vqt, dk, dv = refs
    yh, x, yl, core = place_ref[0], place_ref[1], place_ref[2], place_ref[4]
    low = lax.broadcasted_iota(jnp.int32, (32, 128), 1) < 64

    def row_of(yls, n):
        return pl.multiple_of(((yl ^ yls) * 16 + n) * TOK, TOK)

    def build(n, _):
        for yls in range(2):
            at = row_of(yls, n)
            for m in range(4):
                xs = 2 * (m % 2)
                left = bias_refs[2 * xs + m // 2][yls, n].astype(F32) * LOG2E
                right = bias_refs[2 * xs + 2 + m // 2][yls, n].astype(F32) * LOG2E
                lanes = slice(m * 128, (m + 1) * 128)
                b32[pl.ds(at, 32), lanes] = jnp.where(low, left, swap_halves(right))
                b32[pl.ds(at + 32, 32), lanes] = jnp.where(low, swap_halves(left), right)
        return 0

    lax.fori_loop(0, 16, build, 0)
    acc[...] = jnp.zeros_like(acc) if first else acc_in[...]
    steps = LEN // CHUNK

    homes = [((yh ^ (p // 4)) * 4 + ((x - p % 4) & 3)) * 4 for p in range(ROWS)]

    def queries(lo):
        return jnp.concatenate(
            [recv_ref[pl.ds(at, 4), lo : lo + SUB, :].reshape(TOK, 128) for at in homes], axis=0
        )

    mine = recv_ref[:, :TOK, :].reshape(LEN, 128)
    theirs = other_ref[...].reshape(LEN, 128)
    keys = jnp.where(core == 0, mine, theirs)
    values = jnp.where(core == 0, theirs, mine)
    kq[...] = keys
    vq[...] = values
    kqt[...] = keys.T
    vqt[...] = values.T
    query = queries(TOK)
    cot = queries(TOK + SUB)
    query_t = query.T
    cot_t = cot.T
    dk[...] = jnp.zeros_like(dk)
    dv[...] = jnp.zeros_like(dv)
    lanes = lane_group((QRY, 128))
    subs = lax.broadcasted_iota(jnp.int32, (128, QRY), 0) // D
    zero = jnp.zeros((), BF16)
    out_t, dq_t = [], []
    for i in range(QUAD):
        band = slice(i * D, (i + 1) * D)
        q_m = jnp.where(lanes == i, query, zero)
        c_m = jnp.where(lanes == i, cot, zero)
        qt_m = jnp.where(subs == i, query_t, zero)
        ct_m = jnp.where(subs == i, cot_t, zero)

        def score(c, top, qt_m=qt_m):
            rows = pl.ds(pl.multiple_of(c * CHUNK, CHUNK), CHUNK)
            s = nn(kq[rows, :], qt_m) * (SCALE * LOG2E) + b32[rows, :]
            s_ref[rows, :] = s
            return jnp.maximum(top, jnp.max(s.reshape(CHUNK // 8, 8, QRY), axis=0))

        top = lax.fori_loop(0, steps, score, jnp.full((8, QRY), -3e38, F32), unroll=2)
        top = jnp.max(top, axis=0, keepdims=True)

        def weigh(c, carry, band=band, top=top):
            total, out = carry
            rows = pl.ds(pl.multiple_of(c * CHUNK, CHUNK), CHUNK)
            e = jnp.exp2(s_ref[rows, :] - top)
            s_ref[rows, :] = e
            total = total + jnp.sum(e.reshape(CHUNK // 8, 8, QRY), axis=0)
            out = out + nn(vqt[band, rows], e.astype(BF16))
            return total, out

        total, out = lax.fori_loop(
            0,
            steps,
            weigh,
            (jnp.zeros((8, QRY), F32), jnp.zeros((D, QRY), F32)),
            unroll=2,
        )
        inv = 1.0 / jnp.sum(total, axis=0, keepdims=True)
        out = out * inv
        delta = jnp.sum(cot_t[band].astype(F32) * out, axis=0, keepdims=True)

        def back(c, dq, band=band, inv=inv, delta=delta, q_m=q_m, c_m=c_m, ct_m=ct_m):
            rows = pl.ds(pl.multiple_of(c * CHUNK, CHUNK), CHUNK)
            prob = s_ref[rows, :] * inv
            ds = prob * (nn(vq[rows, :], ct_m) - delta)
            acc[rows, :] += ds
            half = ds.astype(BF16)
            dk[rows, :] += nn(half, q_m)
            dv[rows, :] += nn(prob.astype(BF16), c_m)
            return dq + nn(kqt[band, rows], half)

        dq = lax.fori_loop(0, steps, back, jnp.zeros((D, QRY), F32), unroll=2)
        out_t.append(out)
        dq_t.append(dq * SCALE)
    dq = jnp.concatenate(dq_t, axis=0).T.astype(BF16)
    out = jnp.concatenate(out_t, axis=0).T.astype(BF16)
    for p, at in enumerate(homes):
        part = slice(p * TOK, (p + 1) * TOK)
        back_out[pl.ds(at, 4), TOK : TOK + SUB, :] = dq[part].reshape(4, SUB, 128)
        back_out[pl.ds(at, 4), TOK + SUB :, :] = out[part].reshape(4, SUB, 128)
    key_grad = (dk[...] * SCALE).astype(BF16).reshape(COLS, TOK, 128)
    value_grad = dv[...].astype(BF16).reshape(COLS, TOK, 128)
    back_out[:, :TOK, :] = jnp.where(core == 0, key_grad, value_grad)
    give_out[...] = jnp.where(core == 0, value_grad, key_grad)
    if first:
        return

    def spread(n, _):
        for yls in range(2):
            at = row_of(yls, n)
            for m in range(4):
                xs = 2 * (m % 2)
                lanes = slice(m * 128, (m + 1) * 128)
                top = acc[pl.ds(at, 32), lanes]
                bottom = acc[pl.ds(at + 32, 32), lanes]
                left = jnp.where(low, top, swap_halves(bottom))
                right = jnp.where(low, swap_halves(top), bottom)
                bg_outs[2 * xs + m // 2][yls, n] = left.astype(BF16)
                bg_outs[2 * xs + 2 + m // 2][yls, n] = right.astype(BF16)
        return 0

    lax.fori_loop(0, 16, spread, 0)


def merge_kernel(back_ref, given_ref, out_ref):
    own = back_ref[:, :TOK, :].astype(F32)
    out_ref[:, :TOK, :] = (own + given_ref[...].astype(F32)).astype(BF16)
    out_ref[:, TOK:, :] = back_ref[:, TOK:, :]


def finish_kernel(
    recv_a_ref,
    recv_b_ref,
    gates_ref,
    ograd_ref,
    pair_ref,
    grad_ref,
    wp_ref,
    bg_0_ref,
    bg_1_ref,
    bg_2_ref,
    bg_3_ref,
    pair_out,
    send_out,
    pg,
    gt,
    weight_out,
):
    for q in range(4):
        rows = slice(q * TOK, (q + 1) * TOK)
        recv_ref = recv_b_ref if q % 2 else recv_a_ref
        wide = slice(0, TOK)
        for h in range(H):
            base = (q // 2) * 16 + h * 4
            key = recv_ref[base, wide].astype(F32) + recv_ref[base + 2, wide].astype(F32)
            value = recv_ref[base + 1, wide].astype(F32) + recv_ref[base + 3, wide].astype(F32)
            query = jnp.concatenate(
                [recv_ref[base + j, TOK : TOK + SUB] for j in range(4)],
                axis=0,
            )
            out = jnp.concatenate(
                [recv_ref[base + j, TOK + SUB :] for j in range(4)],
                axis=0,
            ).astype(F32)
            lanes = slice(h * 128, (h + 1) * 128)
            sig = jax.nn.sigmoid(gates_ref[q, :, lanes].astype(F32))
            og = ograd_ref[q, :, lanes].astype(F32)
            gt[rows, lanes] = (sig * out).astype(BF16)
            pg[rows, h * 512 : h * 512 + 128] = query
            pg[rows, h * 512 + 128 : h * 512 + 256] = key.astype(BF16)
            pg[rows, h * 512 + 256 : h * 512 + 384] = value.astype(BF16)
            pg[rows, h * 512 + 384 : h * 512 + 512] = (og * out * sig * (1.0 - sig)).astype(BF16)
    wp = wp_ref[...]
    group = lane_group(wp.shape)
    zero = jnp.zeros((), BF16)
    grads = pg[...]
    gated = gt[...]
    for r in range(QUAD):
        part = nt(grads, jnp.where(group == r, wp, zero)).astype(BF16)
        for q in range(4):
            pair_out[4 * q + r] = part[q * TOK : (q + 1) * TOK]
    turned = grads.T
    gated_t = gated.T
    for r in range(QUAD):
        pair_r = jnp.concatenate([pair_ref[4 * q + r] for q in range(4)], axis=0)
        grad_r = jnp.concatenate([grad_ref[4 * q + r] for q in range(4)], axis=0)
        for n in range(16):
            at = n * 128 + r * D
            piece = nn(turned[at : at + D], pair_r) * (1.0 / LEN)
            if r == 0:
                weight_out[n * D : (n + 1) * D] = piece
            else:
                weight_out[n * D : (n + 1) * D] += piece
        for n in range(4):
            at = n * 128 + r * D
            piece = nn(gated_t[at : at + D], grad_r) * (1.0 / LEN)
            where = slice(512 + n * D, 512 + (n + 1) * D)
            if r == 0:
                weight_out[where] = piece
            else:
                weight_out[where] += piece


    weight_out[640:] = jnp.zeros((128, 128), F32)
    bias_sum = bg_0_ref[...].astype(F32)
    for ref in (bg_1_ref, bg_2_ref, bg_3_ref):
        bias_sum = bias_sum + ref[...].astype(F32)
    send_out[:, :32, :] = bias_sum.astype(BF16)
    weights = weight_out[...]
    high = weights.astype(BF16)
    send_out[:, 32:80, :] = high.reshape(16, 48, 128)
    send_out[:, 80:, :] = (weights - high.astype(F32)).astype(BF16).reshape(16, 48, 128)


def whole():
    return pl.BlockSpec(memory_space=pltpu.VMEM)


def scalar():
    return pl.BlockSpec(memory_space=pltpu.SMEM)


def call(kernel, in_specs, outs, scratch=(), flops=0, moved=0):
    return pl.pallas_call(
        kernel,
        out_shape=outs,
        in_specs=in_specs,
        out_specs=jax.tree.map(lambda _: whole(), outs),
        scratch_shapes=list(scratch),
        compiler_params=pltpu.CompilerParams(vmem_limit_bytes=VMEM_LIMIT),
        cost_estimate=pl.CostEstimate(flops=flops, bytes_accessed=moved, transcendentals=0),
    )


def shape(dims, dtype=BF16):
    return jax.ShapeDtypeStruct(dims, dtype)


def query_order():
    perm = np.zeros((256, 256), np.float32)
    for s in range(4):
        for j in range(4):
            for t in range(SUB):
                perm[s * 64 + j * SUB + t, j * 64 + s * SUB + t] = 1.0
    return perm


def widen(groups):
    source = lax.broadcasted_iota(jnp.int32, (groups * D, groups * 128), 0)
    target = lax.broadcasted_iota(jnp.int32, (groups * D, groups * 128), 1)
    same = (source // D == target // 128) & (source % D == target % D)
    return same.astype(BF16)


def shift(x, axis, step):
    count = {"x": 4, "c": 2}[axis]
    return lax.ppermute(x, axis, [(n, (n + step) % count) for n in range(count)])


def flip_y(x, bits):
    return lax.ppermute(x, ("yh", "yl"), [(n, n ^ bits) for n in range(4)])


PIECE = (32, 128)
HALF = (2, 16) + PIECE


def gather_bias(own):
    ys = [own] + [flip_y(own, bits) for bits in range(1, 4)]
    here = [jnp.stack(ys[:2]), jnp.stack(ys[2:])]
    left = [shift(a, "x", 1) for a in here]
    right = [shift(a, "x", -1) for a in here]
    far = [shift(right[0], "x", -1), shift(left[1], "x", 1)]
    return here + left + far + right


def total(*terms):
    return sum(t.astype(F32) for t in terms).astype(BF16)


def scatter_bias(parts):
    here, left, far, right = parts[:2], parts[2:4], parts[4:6], parts[6:]
    from_left_b = shift(right[1], "x", 1)
    from_right_a = shift(left[0], "x", -1)
    through_a = shift(far[0], "x", 1)
    through_b = shift(far[1], "x", -1)
    from_left_a = shift(total(right[0], through_a), "x", 1)
    from_right_b = shift(total(left[1], through_b), "x", -1)
    sum_a = total(here[0], from_left_a, from_right_a)
    sum_b = total(here[1], from_left_b, from_right_b)
    return sum_a[0], flip_y(sum_a[1], 1), flip_y(sum_b[0], 2), flip_y(sum_b[1], 3)


CHUNK_ROWS = TOK + 2 * SUB


def attend(first, place, recv, bias, acc=()):
    other = shift(recv[:, :TOK], "c", 1)
    big = (LEN, QRY)
    scratch = [pltpu.VMEM(big, F32), pltpu.VMEM(big, F32)]
    scratch += [pltpu.VMEM((LEN, 128), BF16)] * 2 + [pltpu.VMEM((128, LEN), BF16)] * 2
    scratch += [pltpu.VMEM((LEN, 128), F32)] * 2
    outs = (shape((COLS, CHUNK_ROWS, 128)), shape((COLS, TOK, 128)))
    if first:
        outs += (shape(big, F32),)
    else:
        outs += (shape(HALF),) * 8
        scratch = [pltpu.VMEM(big, F32)] + scratch
    back, give, *rest = call(
        lambda *refs: attend_kernel(first, *refs),
        [scalar()] + [whole()] * (10 + len(acc)),
        outs,
        scratch,
        flops=25_000_000_000,
        moved=10_000_000,
    )(place, recv, other, *bias, *acc)
    given = shift(give, "c", 1)
    merged = call(
        merge_kernel, [whole()] * 2, shape((COLS, CHUNK_ROWS, 128)), moved=2_000_000
    )(back, given)
    return merged, rest


def on_device(pair_rep, w_proj, bias_logits, chain_lengths, w_out, grad_out):
    col = ("yl", "z", "c")
    plane = ("yh", "x", "yl")
    line = ("z", "c")
    place = jnp.stack([lax.axis_index(a) for a in ("yh", "x", "yl", "z", "c")]).astype(jnp.int32)
    perm = jnp.asarray(query_order(), BF16)

    packed = call(
        bias_pack_kernel, [scalar(), scalar(), whole(), whole()], shape((16,) + PIECE)
    )(place, chain_lengths, perm, jnp.swapaxes(bias_logits, 1, 2))
    bias = gather_bias(lax.all_to_all(packed, line, 0, 0, tiled=True))
    wp = jnp.dot(w_proj, widen(16), preferred_element_type=F32).astype(BF16)
    wo = jnp.dot(w_out.T, widen(4), preferred_element_type=F32).astype(BF16)
    part = shape((COLS, CHUNK_ROWS, 128))
    send_a, send_b, gates, ograd = call(
        project_kernel,
        [whole()] * 4,
        (part, part, shape((4, TOK, 512)), shape((4, TOK, 512))),
        flops=700_000_000,
        moved=6_000_000,
    )(pair_rep, grad_out, wp, wo)
    recv_a = lax.all_to_all(send_a, col, 0, 0, tiled=True)
    recv_b = lax.all_to_all(send_b, col, 0, 0, tiled=True)
    back_a, acc = attend(True, place, recv_a, bias)
    home_a = lax.all_to_all(back_a, col, 0, 0, tiled=True)
    back_b, bg = attend(False, place, recv_b, bias, acc)
    home_b = lax.all_to_all(back_b, col, 0, 0, tiled=True)
    pair_grad, pieces = call(
        finish_kernel,
        [whole()] * 11,
        (shape((16, TOK, 128)), shape((16, 128, 128))),
        [
            pltpu.VMEM((256, 2048), BF16),
            pltpu.VMEM((256, 512), BF16),
            pltpu.VMEM((768, 128), F32),
        ],
        flops=1_000_000_000,
        moved=4_000_000,
    )(home_a, home_b, gates, ograd, pair_rep, grad_out, wp, *scatter_bias(bg))
    pieces = lax.all_to_all(pieces, line, 0, 0, tiled=True)
    bias_grad = call(bias_unpack_kernel, [whole()] * 2, shape((H, TOK, 256), F32))(perm, pieces)
    share = jnp.sum(pieces[:, 32:].astype(F32), axis=0)
    share = share[:48] + share[48:]
    share = lax.all_to_all(
        jnp.broadcast_to(share[None], (16, 48, 128)), plane, 0, 0, tiled=True
    )
    share = jnp.sum(share, axis=0).astype(BF16)
    every = lax.all_to_all(
        jnp.broadcast_to(share[None], (16, 48, 128)), line, 0, 0, tiled=True
    )
    every = every.reshape(768, 128).astype(F32)
    return (pair_grad, jnp.swapaxes(bias_grad, 1, 2), every[:512].T, every[512:640])


def solution(mesh):
    fine = Mesh(mesh.devices.reshape(2, 4, 2, 8, 2), ("yh", "x", "yl", "z", "c"))
    row = ("yh", "x")
    col = ("yl", "z", "c")
    return jax.shard_map(
        on_device,
        mesh=fine,
        in_specs=(
            P(row, col, None),
            P(),
            P(None, row, col),
            P(),
            P(),
            P(row, col, None),
        ),
        out_specs=(P(row, col, None), P(None, row, col), P(), P()),
        check_vma=False,
    )
```

```python
import jax
import jax.numpy as jnp
import numpy as np
from jax import lax
from jax.experimental import pallas as pl
from jax.experimental.pallas import tpu as pltpu
from jax.sharding import Mesh
from jax.sharding import PartitionSpec as P

H = 4
D = 32
CHAINS = 4
NEG_BIG = -1e30
LOG2E = 1.4426950408889634
SCALE = D ** (-0.5)
F32 = jnp.float32
BF16 = jnp.bfloat16
QUAD = 4
TOK = 64
SUB = 16
COLS = 32
ROWS = 8
LEN = TOK * COLS
QRY = SUB * COLS
VMEM_LIMIT = 56 * 1024 * 1024


def dot(a, b, dims):
    return lax.dot_general(a, b, (dims, ((), ())), preferred_element_type=F32)


def nn(a, b):
    return dot(a, b, ((1,), (0,)))


def nt(a, b):
    return dot(a, b, ((1,), (1,)))


def tn(a, b):
    return dot(a, b, ((0,), (0,)))


def lane_group(shape):
    return (lax.broadcasted_iota(jnp.int32, shape, 1) // D) % QUAD


def swap_halves(x):
    return jnp.concatenate([x[:, TOK:], x[:, :TOK]], axis=1)


def bias_pack_kernel(place_ref, chain_ref, perm_ref, bias_ref, out_ref):
    block = (place_ref[2] * 8 + place_ref[3]) * 2 + place_ref[4]
    per_chain = COLS // CHAINS
    limit = chain_ref[block // per_chain] - (block % per_chain) * TOK
    low = lax.broadcasted_iota(jnp.int32, (32, 128), 1) < 64
    valid = lax.broadcasted_iota(jnp.int32, (TOK, 256), 0) < limit
    for h in range(H):
        ordered = jnp.where(valid, nn(bias_ref[h], perm_ref[...]), NEG_BIG)
        for m in range(2):
            top = ordered[:32, m * 128 : (m + 1) * 128]
            bottom = ordered[32:, m * 128 : (m + 1) * 128]
            out_ref[h * 4 + 2 * m] = jnp.where(low, top, swap_halves(bottom)).astype(BF16)
            out_ref[h * 4 + 2 * m + 1] = jnp.where(low, swap_halves(top), bottom).astype(BF16)


def bias_unpack_kernel(perm_ref, parts_ref, out_ref):
    low = lax.broadcasted_iota(jnp.int32, (32, 128), 1) < 64
    for h in range(H):
        tops, bottoms = [], []
        for m in range(2):
            first = parts_ref[h * 4 + 2 * m, :32].astype(F32)
            second = parts_ref[h * 4 + 2 * m + 1, :32].astype(F32)
            tops.append(jnp.where(low, first, swap_halves(second)))
            bottoms.append(jnp.where(low, swap_halves(first), second))
        ordered = jnp.concatenate(
            [jnp.concatenate(tops, axis=1), jnp.concatenate(bottoms, axis=1)], axis=0
        ).astype(BF16)
        out_ref[h] = nt(ordered, perm_ref[...])


def project_kernel(
    pair_ref, grad_ref, wp_ref, wo_ref, send_a_ref, send_b_ref, gates_ref, ograd_ref
):
    wp = wp_ref[...]
    wo = wo_ref[...]
    group_p = lane_group(wp.shape)
    group_o = lane_group(wo.shape)
    zero = jnp.zeros((), BF16)
    wide_p = jnp.concatenate([jnp.where(group_p == r, wp, zero) for r in range(QUAD)], axis=0)
    wide_o = jnp.concatenate([jnp.where(group_o == r, wo, zero) for r in range(QUAD)], axis=0)

    def quads(ref):
        return jnp.concatenate(
            [
                jnp.concatenate([ref[4 * q + r] for r in range(QUAD)], axis=1)
                for q in range(4)
            ],
            axis=0,
        )

    proj = nn(quads(pair_ref), wide_p).astype(BF16)
    ograd = nn(quads(grad_ref), wide_o).astype(BF16)
    for q in range(4):
        rows = slice(q * TOK, (q + 1) * TOK)
        send_ref = send_b_ref if q // 2 else send_a_ref
        for h in range(H):
            query, key, value, gate = [
                proj[rows, h * 512 + p * 128 : h * 512 + (p + 1) * 128] for p in range(4)
            ]
            og = ograd[rows, h * 128 : (h + 1) * 128]
            gates_ref[q, :, h * 128 : (h + 1) * 128] = gate
            ograd_ref[q, :, h * 128 : (h + 1) * 128] = og
            cot = (og.astype(F32) * jax.nn.sigmoid(gate.astype(F32))).astype(BF16)
            for j in range(4):
                dest = (q % 2) * 16 + h * 4 + j
                send_ref[dest, :TOK] = value if j % 2 else key
                part = slice(j * SUB, (j + 1) * SUB)
                send_ref[dest, TOK : TOK + SUB] = query[part]
                send_ref[dest, TOK + SUB :] = cot[part]


CHUNK = 512
KEYS = 3 * LEN // 4


def attend_kernel(first, place_ref, chain_ref, recv_ref, other_ref, *refs):
    bias_refs, refs = refs[:8], refs[8:]
    if first:
        back_out, give_out, acc, *refs = refs
    else:
        acc_in, back_out, give_out, *refs = refs
        bg_outs, (acc, *refs) = refs[:8], refs[8:]
    b32, s_ref, kf, vf, kq, vq, kqt, vqt, dk, dv = refs
    yh, x, yl, core = place_ref[0], place_ref[1], place_ref[2], place_ref[4]
    low = lax.broadcasted_iota(jnp.int32, (32, 128), 1) < 64
    lens = [chain_ref[n] for n in range(CHAINS)]
    starts = [0, lens[0], lens[0] + lens[1], lens[0] + lens[1] + lens[2]]

    def pick(values, n):
        return jnp.where(
            n < 2, jnp.where(n == 0, values[0], values[1]), jnp.where(n == 2, values[2], values[3])
        )

    def place_of(t):
        return pick(starts, t // 8) + (t % 8) * TOK

    def build(t, _):
        at = place_of(t)
        yls, n = (t // 16) ^ yl, t % 16
        for m in range(4):
            xs = 2 * (m % 2)
            left = bias_refs[2 * xs + m // 2][yls, n].astype(F32) * LOG2E
            right = bias_refs[2 * xs + 2 + m // 2][yls, n].astype(F32) * LOG2E
            b32[m, pl.ds(at, 32), :] = jnp.where(low, left, swap_halves(right))
            b32[m, pl.ds(at + 32, 32), :] = jnp.where(low, swap_halves(left), right)
        mine = recv_ref[t, :TOK, :].astype(F32)
        theirs = other_ref[t].astype(F32)
        kf[pl.ds(at, TOK), :] = jnp.where(core == 0, mine, theirs)
        vf[pl.ds(at, TOK), :] = jnp.where(core == 0, theirs, mine)
        return 0

    lax.fori_loop(0, COLS, build, 0, unroll=8)
    acc[:, :KEYS, :] = jnp.zeros((4, KEYS, 128), F32) if first else acc_in[...]
    keys = kf[:KEYS, :].astype(BF16)
    values = vf[:KEYS, :].astype(BF16)
    kq[...] = keys
    vq[...] = values
    kqt[...] = keys.T
    vqt[...] = values.T

    homes = [((yh ^ (p // 4)) * 4 + ((x - p % 4) & 3)) * 4 for p in range(ROWS)]

    def queries(lo):
        return jnp.concatenate(
            [recv_ref[pl.ds(at, 4), lo : lo + SUB, :].reshape(TOK, 128) for at in homes], axis=0
        )

    query = queries(TOK)
    cot = queries(TOK + SUB)
    query_t = query.T
    cot_t = cot.T
    lanes = lane_group((QRY, 128))
    subs = lax.broadcasted_iota(jnp.int32, (128, QRY), 0) // D
    zero = jnp.zeros((), BF16)
    chunks = [slice(c * CHUNK, (c + 1) * CHUNK) for c in range(KEYS // CHUNK)]
    out_t, dq_t = [], []
    for i in range(QUAD):
        band = slice(i * D, (i + 1) * D)
        q_m = jnp.where(lanes == i, query, zero)
        c_m = jnp.where(lanes == i, cot, zero)
        qt_m = jnp.where(subs == i, query_t, zero)
        ct_m = jnp.where(subs == i, cot_t, zero)
        top = jnp.full((8, QRY), -3e38, F32)
        for rows in chunks:
            s = nn(kq[rows, :], qt_m) * (SCALE * LOG2E)
            s = s + jnp.concatenate([b32[m, rows, :] for m in range(4)], axis=1)
            s_ref[rows, :] = s
            top = jnp.maximum(top, jnp.max(s.reshape(CHUNK // 8, 8, QRY), axis=0))
        top = jnp.max(top, axis=0, keepdims=True)
        total = jnp.zeros((8, QRY), F32)
        out = jnp.zeros((D, QRY), F32)
        for rows in chunks:
            e = jnp.exp2(s_ref[rows, :] - top)
            s_ref[rows, :] = e
            total = total + jnp.sum(e.reshape(CHUNK // 8, 8, QRY), axis=0)
            out = out + nn(vqt[band, rows], e.astype(BF16))
        inv = 1.0 / jnp.sum(total, axis=0, keepdims=True)
        out = out * inv
        delta = jnp.sum(cot_t[band].astype(F32) * out, axis=0, keepdims=True)
        dq = jnp.zeros((D, QRY), F32)
        for rows in chunks:
            prob = s_ref[rows, :] * inv
            ds = prob * (nn(vq[rows, :], ct_m) - delta)
            for m in range(4):
                acc[m, rows, :] += ds[:, m * 128 : (m + 1) * 128]
            half = ds.astype(BF16)
            key_part = nn(half, q_m)
            value_part = nn(prob.astype(BF16), c_m)
            if i:
                dk[rows, :] += key_part
                dv[rows, :] += value_part
            else:
                dk[rows, :] = key_part
                dv[rows, :] = value_part
            dq = dq + nn(kqt[band, rows], half)
        out_t.append(out)
        dq_t.append(dq * SCALE)
    dq = jnp.concatenate(dq_t, axis=0).T.astype(BF16)
    out = jnp.concatenate(out_t, axis=0).T.astype(BF16)
    for p, at in enumerate(homes):
        part = slice(p * TOK, (p + 1) * TOK)
        back_out[pl.ds(at, 4), TOK : TOK + SUB, :] = dq[part].reshape(4, SUB, 128)
        back_out[pl.ds(at, 4), TOK + SUB :, :] = out[part].reshape(4, SUB, 128)

    def spread(t, _):
        at = place_of(t)
        here = lax.broadcasted_iota(jnp.int32, (TOK, 128), 0) < pick(lens, t // 8) - (t % 8) * TOK
        key_grad = jnp.where(here, dk[pl.ds(at, TOK), :] * SCALE, 0.0).astype(BF16)
        value_grad = jnp.where(here, dv[pl.ds(at, TOK), :], 0.0).astype(BF16)
        back_out[t, :TOK, :] = jnp.where(core == 0, key_grad, value_grad)
        give_out[t] = jnp.where(core == 0, value_grad, key_grad)
        if first:
            return 0
        yls, n = (t // 16) ^ yl, t % 16
        for m in range(4):
            xs = 2 * (m % 2)
            top = jnp.where(here[:32], acc[m, pl.ds(at, 32), :], 0.0)
            bottom = jnp.where(here[32:], acc[m, pl.ds(at + 32, 32), :], 0.0)
            left = jnp.where(low, top, swap_halves(bottom))
            right = jnp.where(low, swap_halves(top), bottom)
            bg_outs[2 * xs + m // 2][yls, n] = left.astype(BF16)
            bg_outs[2 * xs + 2 + m // 2][yls, n] = right.astype(BF16)
        return 0

    lax.fori_loop(0, COLS, spread, 0, unroll=8)


def merge_kernel(back_ref, given_ref, out_ref):
    own = back_ref[:, :TOK, :].astype(F32)
    out_ref[:, :TOK, :] = (own + given_ref[...].astype(F32)).astype(BF16)
    out_ref[:, TOK:, :] = back_ref[:, TOK:, :]


def merge(back, given):
    def block(rows):
        return pl.BlockSpec((COLS // 4, rows, 128), lambda n: (n, 0, 0))

    return pl.pallas_call(
        merge_kernel,
        grid=(4,),
        out_shape=shape((COLS, CHUNK_ROWS, 128)),
        in_specs=[block(CHUNK_ROWS), block(TOK)],
        out_specs=block(CHUNK_ROWS),
        cost_estimate=pl.CostEstimate(flops=0, bytes_accessed=2_000_000, transcendentals=0),
    )(back, given)


def finish_kernel(part, recv_ref, gates_ref, ograd_ref, pair_ref, grad_ref, wp_ref, *refs):
    if part:
        weight_in, *bias_refs, pair_out, send_out, pg, gt, weight_out = refs
    else:
        pair_out, weight_out, pg, gt = refs
    quads = [2 * part, 2 * part + 1]
    for n, q in enumerate(quads):
        rows = slice(n * TOK, (n + 1) * TOK)
        for h in range(H):
            base = n * 16 + h * 4
            key = recv_ref[base, :TOK].astype(F32) + recv_ref[base + 2, :TOK].astype(F32)
            value = recv_ref[base + 1, :TOK].astype(F32) + recv_ref[base + 3, :TOK].astype(F32)
            query = jnp.concatenate(
                [recv_ref[base + j, TOK : TOK + SUB] for j in range(4)], axis=0
            )
            out = jnp.concatenate(
                [recv_ref[base + j, TOK + SUB :] for j in range(4)], axis=0
            ).astype(F32)
            lanes = slice(h * 128, (h + 1) * 128)
            sig = jax.nn.sigmoid(gates_ref[q, :, lanes].astype(F32))
            og = ograd_ref[q, :, lanes].astype(F32)
            gt[rows, lanes] = (sig * out).astype(BF16)
            pg[rows, h * 512 : h * 512 + 128] = query
            pg[rows, h * 512 + 128 : h * 512 + 256] = key.astype(BF16)
            pg[rows, h * 512 + 256 : h * 512 + 384] = value.astype(BF16)
            pg[rows, h * 512 + 384 : h * 512 + 512] = (og * out * sig * (1.0 - sig)).astype(BF16)
    wp = wp_ref[...]
    group = lane_group(wp.shape)
    zero = jnp.zeros((), BF16)
    grads = pg[...]
    gated = gt[...]
    for r in range(QUAD):
        pair_grad = nt(grads, jnp.where(group == r, wp, zero)).astype(BF16)
        for n in range(2):
            pair_out[4 * n + r] = pair_grad[n * TOK : (n + 1) * TOK]
    turned = grads.T
    gated_t = gated.T
    for r in range(QUAD):
        pair_r = jnp.concatenate([pair_ref[4 * q + r] for q in quads], axis=0)
        grad_r = jnp.concatenate([grad_ref[4 * q + r] for q in quads], axis=0)
        for n in range(20):
            source, other = (turned, pair_r) if n < 16 else (gated_t, grad_r)
            at = (n % 16) * 128 + r * D
            piece = nn(source[at : at + D], other) * (1.0 / LEN)
            rows = slice(n * D, (n + 1) * D)
            if r:
                weight_out[rows] += piece
            elif part:
                weight_out[rows] = weight_in[rows] + piece
            else:
                weight_out[rows] = piece
    if not part:
        return
    weight_out[640:] = jnp.zeros((128, 128), F32)
    bias_sum = bias_refs[0][...].astype(F32)
    for ref in bias_refs[1:]:
        bias_sum = bias_sum + ref[...].astype(F32)
    send_out[:, :32, :] = bias_sum.astype(BF16)
    send_out[:, 32:, :] = weight_out[...].astype(BF16).reshape(16, 48, 128)


def finish(part, home, gates, ograd, pair_rep, grad_out, wp, *more):
    last = shape((16, 80, 128)) if part else shape((640, 128), F32)
    scratch = [pltpu.VMEM((128, 2048), BF16), pltpu.VMEM((128, 512), BF16)]
    if part:
        scratch.append(pltpu.VMEM((768, 128), F32))
    return call(
        lambda *refs: finish_kernel(part, *refs),
        [whole()] * (6 + len(more)),
        (shape((8, TOK, 128)), last),
        scratch,
        flops=1_000_000_000,
        moved=3_000_000,
    )(home, gates, ograd, pair_rep, grad_out, wp, *more)


def whole():
    return pl.BlockSpec(memory_space=pltpu.VMEM)


def scalar():
    return pl.BlockSpec(memory_space=pltpu.SMEM)


def call(kernel, in_specs, outs, scratch=(), flops=0, moved=0):
    return pl.pallas_call(
        kernel,
        out_shape=outs,
        in_specs=in_specs,
        out_specs=jax.tree.map(lambda _: whole(), outs),
        scratch_shapes=list(scratch),
        compiler_params=pltpu.CompilerParams(vmem_limit_bytes=VMEM_LIMIT),
        cost_estimate=pl.CostEstimate(flops=flops, bytes_accessed=moved, transcendentals=0),
    )


def shape(dims, dtype=BF16):
    return jax.ShapeDtypeStruct(dims, dtype)


def query_order():
    perm = np.zeros((256, 256), np.float32)
    for s in range(4):
        for j in range(4):
            for t in range(SUB):
                perm[s * 64 + j * SUB + t, j * 64 + s * SUB + t] = 1.0
    return perm


def widen(groups):
    source = lax.broadcasted_iota(jnp.int32, (groups * D, groups * 128), 0)
    target = lax.broadcasted_iota(jnp.int32, (groups * D, groups * 128), 1)
    same = (source // D == target // 128) & (source % D == target % D)
    return same.astype(BF16)


def shift(x, axis, step):
    count = {"x": 4, "c": 2}[axis]
    return lax.ppermute(x, axis, [(n, (n + step) % count) for n in range(count)])


def flip_y(x, bits):
    return lax.ppermute(x, ("yh", "yl"), [(n, n ^ bits) for n in range(4)])


PIECE = (32, 128)
HALF = (2, 16) + PIECE


def gather_bias(own):
    ys = [own] + [flip_y(own, bits) for bits in range(1, 4)]
    here = [jnp.stack(ys[:2]), jnp.stack(ys[2:])]
    left = [shift(a, "x", 1) for a in here]
    right = [shift(a, "x", -1) for a in here]
    far = [shift(right[0], "x", -1), shift(left[1], "x", 1)]
    return here + left + far + right


def total(*terms):
    return sum(t.astype(F32) for t in terms).astype(BF16)


def scatter_bias(parts):
    here, left, far, right = parts[:2], parts[2:4], parts[4:6], parts[6:]
    from_left_b = shift(right[1], "x", 1)
    from_right_a = shift(left[0], "x", -1)
    through_a = shift(far[0], "x", 1)
    through_b = shift(far[1], "x", -1)
    from_left_a = shift(total(right[0], through_a), "x", 1)
    from_right_b = shift(total(left[1], through_b), "x", -1)
    sum_a = total(here[0], from_left_a, from_right_a)
    sum_b = total(here[1], from_left_b, from_right_b)
    return sum_a[0], flip_y(sum_a[1], 1), flip_y(sum_b[0], 2), flip_y(sum_b[1], 3)


CHUNK_ROWS = TOK + 2 * SUB


def attend_call(first, place, chain_lengths, recv, other, bias, acc):
    packed = pltpu.VMEM((4, LEN, 128), F32)
    tall = [pltpu.VMEM((LEN, 128), F32)] * 2
    scratch = [packed, pltpu.VMEM((KEYS, QRY), F32)] + tall
    scratch += [pltpu.VMEM((KEYS, 128), BF16)] * 2 + [pltpu.VMEM((128, KEYS), BF16)] * 2 + tall
    outs = (shape((COLS, CHUNK_ROWS, 128)), shape((COLS, TOK, 128)))
    if first:
        outs += (shape((4, KEYS, 128), F32),)
    else:
        outs += (shape(HALF),) * 8
        scratch = [packed] + scratch
    return call(
        lambda *refs: attend_kernel(first, *refs),
        [scalar()] * 2 + [whole()] * (10 + len(acc)),
        outs,
        scratch,
        flops=25_000_000_000,
        moved=10_000_000,
    )(place, chain_lengths, recv, other, *bias, *acc)


def attend(first, place, chain_lengths, recv, bias, acc=()):
    other = shift(recv[:, :TOK], "c", 1)
    back, give, *rest = attend_call(first, place, chain_lengths, recv, other, bias, acc)
    given = shift(give, "c", 1)
    merged = merge(back, given)
    return merged, rest


def on_device(pair_rep, w_proj, bias_logits, chain_lengths, w_out, grad_out):
    col = ("yl", "z", "c")
    plane = ("yh", "x", "yl")
    line = ("z", "c")
    place = jnp.stack([lax.axis_index(a) for a in ("yh", "x", "yl", "z", "c")]).astype(jnp.int32)
    perm = jnp.asarray(query_order(), BF16)

    packed = call(
        bias_pack_kernel, [scalar(), scalar(), whole(), whole()], shape((16,) + PIECE)
    )(place, chain_lengths, perm, jnp.swapaxes(bias_logits, 1, 2))
    bias = gather_bias(lax.all_to_all(packed, line, 0, 0, tiled=True))
    wp = jnp.dot(w_proj, widen(16), preferred_element_type=F32).astype(BF16)
    wo = jnp.dot(w_out.T, widen(4), preferred_element_type=F32).astype(BF16)
    part = shape((COLS, CHUNK_ROWS, 128))
    send_a, send_b, gates, ograd = call(
        project_kernel,
        [whole()] * 4,
        (part, part, shape((4, TOK, 512)), shape((4, TOK, 512))),
        flops=700_000_000,
        moved=6_000_000,
    )(pair_rep, grad_out, wp, wo)
    recv_a = lax.all_to_all(send_a, col, 0, 0, tiled=True)
    recv_b = lax.all_to_all(send_b, col, 0, 0, tiled=True)
    back_a, acc = attend(True, place, chain_lengths, recv_a, bias)
    home_a = lax.all_to_all(back_a, col, 0, 0, tiled=True)
    back_b, bg = attend(False, place, chain_lengths, recv_b, bias, acc)
    home_b = lax.all_to_all(back_b, col, 0, 0, tiled=True)
    shared = (gates, ograd, pair_rep, grad_out, wp)
    pair_a, weights = finish(0, home_a, *shared)
    pair_b, pieces = finish(1, home_b, *shared, weights, *scatter_bias(bg))
    pair_grad = jnp.concatenate([pair_a, pair_b], axis=0)
    pieces = lax.all_to_all(pieces, line, 0, 0, tiled=True)
    bias_grad = call(bias_unpack_kernel, [whole()] * 2, shape((H, TOK, 256), F32))(perm, pieces)
    share = jnp.sum(pieces[:, 32:].astype(F32), axis=0)
    share = lax.all_to_all(
        jnp.broadcast_to(share[None], (16, 48, 128)), plane, 0, 0, tiled=True
    )
    share = jnp.sum(share, axis=0).astype(BF16)
    every = lax.all_to_all(
        jnp.broadcast_to(share[None], (16, 48, 128)), line, 0, 0, tiled=True
    )
    every = every.reshape(768, 128).astype(F32)
    return (pair_grad, jnp.swapaxes(bias_grad, 1, 2), every[:512].T, every[512:640])


def solution(mesh):
    fine = Mesh(mesh.devices.reshape(2, 4, 2, 8, 2), ("yh", "x", "yl", "z", "c"))
    row = ("yh", "x")
    col = ("yl", "z", "c")
    return jax.shard_map(
        on_device,
        mesh=fine,
        in_specs=(
            P(row, col, None),
            P(),
            P(None, row, col),
            P(),
            P(),
            P(row, col, None),
        ),
        out_specs=(P(row, col, None), P(None, row, col), P(), P()),
        check_vma=False,
    )
```

```python
import jax
import jax.numpy as jnp
import numpy as np
from jax import lax
from jax.experimental import pallas as pl
from jax.experimental.pallas import tpu as pltpu
from jax.sharding import Mesh
from jax.sharding import PartitionSpec as P

H = 4
D = 32
CHAINS = 4
NEG_BIG = -1e30
LOG2E = 1.4426950408889634
SCALE = D ** (-0.5)
F32 = jnp.float32
BF16 = jnp.bfloat16
QUAD = 4
TOK = 64
SUB = 16
COLS = 32
ROWS = 8
LEN = TOK * COLS
QRY = SUB * COLS
VMEM_LIMIT = 56 * 1024 * 1024


def dot(a, b, dims):
    return lax.dot_general(a, b, (dims, ((), ())), preferred_element_type=F32)


def nn(a, b):
    return dot(a, b, ((1,), (0,)))


def nt(a, b):
    return dot(a, b, ((1,), (1,)))


def tn(a, b):
    return dot(a, b, ((0,), (0,)))


def lane_group(shape):
    return (lax.broadcasted_iota(jnp.int32, shape, 1) // D) % QUAD


def swap_halves(x):
    return jnp.concatenate([x[:, TOK:], x[:, :TOK]], axis=1)


def bias_pack_kernel(place_ref, chain_ref, perm_ref, bias_ref, out_ref):
    block = (place_ref[2] * 8 + place_ref[3]) * 2 + place_ref[4]
    per_chain = COLS // CHAINS
    limit = chain_ref[block // per_chain] - (block % per_chain) * TOK
    low = lax.broadcasted_iota(jnp.int32, (32, 128), 1) < 64
    valid = lax.broadcasted_iota(jnp.int32, (TOK, 256), 0) < limit
    for h in range(H):
        ordered = jnp.where(valid, nn(bias_ref[h], perm_ref[...]), NEG_BIG)
        for m in range(2):
            top = ordered[:32, m * 128 : (m + 1) * 128]
            bottom = ordered[32:, m * 128 : (m + 1) * 128]
            out_ref[h * 4 + 2 * m] = jnp.where(low, top, swap_halves(bottom)).astype(BF16)
            out_ref[h * 4 + 2 * m + 1] = jnp.where(low, swap_halves(top), bottom).astype(BF16)


def bias_unpack_kernel(perm_ref, parts_ref, out_ref):
    low = lax.broadcasted_iota(jnp.int32, (32, 128), 1) < 64
    for h in range(H):
        tops, bottoms = [], []
        for m in range(2):
            first = parts_ref[h * 4 + 2 * m, :32].astype(F32)
            second = parts_ref[h * 4 + 2 * m + 1, :32].astype(F32)
            tops.append(jnp.where(low, first, swap_halves(second)))
            bottoms.append(jnp.where(low, swap_halves(first), second))
        ordered = jnp.concatenate(
            [jnp.concatenate(tops, axis=1), jnp.concatenate(bottoms, axis=1)], axis=0
        ).astype(BF16)
        out_ref[h] = nt(ordered, perm_ref[...])


def project_kernel(
    pair_ref, grad_ref, wp_ref, wo_ref, send_a_ref, send_b_ref, gates_ref, ograd_ref
):
    wp = wp_ref[...]
    wo = wo_ref[...]
    group_p = lane_group(wp.shape)
    group_o = lane_group(wo.shape)
    zero = jnp.zeros((), BF16)
    wide_p = jnp.concatenate([jnp.where(group_p == r, wp, zero) for r in range(QUAD)], axis=0)
    wide_o = jnp.concatenate([jnp.where(group_o == r, wo, zero) for r in range(QUAD)], axis=0)

    def quads(ref):
        return jnp.concatenate(
            [
                jnp.concatenate([ref[4 * q + r] for r in range(QUAD)], axis=1)
                for q in range(4)
            ],
            axis=0,
        )

    proj = nn(quads(pair_ref), wide_p).astype(BF16)
    ograd = nn(quads(grad_ref), wide_o).astype(BF16)
    for q in range(4):
        rows = slice(q * TOK, (q + 1) * TOK)
        send_ref = send_b_ref if q // 2 else send_a_ref
        for h in range(H):
            query, key, value, gate = [
                proj[rows, h * 512 + p * 128 : h * 512 + (p + 1) * 128] for p in range(4)
            ]
            og = ograd[rows, h * 128 : (h + 1) * 128]
            gates_ref[q, :, h * 128 : (h + 1) * 128] = gate
            ograd_ref[q, :, h * 128 : (h + 1) * 128] = og
            cot = (og.astype(F32) * jax.nn.sigmoid(gate.astype(F32))).astype(BF16)
            for j in range(4):
                dest = (q % 2) * 16 + h * 4 + j
                send_ref[dest, :TOK] = value if j % 2 else key
                part = slice(j * SUB, (j + 1) * SUB)
                send_ref[dest, TOK : TOK + SUB] = query[part]
                send_ref[dest, TOK + SUB :] = cot[part]


CHUNK = 512
KEYS = 3 * LEN // 4


def attend_kernel(first, place_ref, chain_ref, recv_ref, other_ref, *refs):
    bias_refs, refs = refs[:5], refs[5:]
    if first:
        back_out, give_out, acc, *refs = refs
    else:
        acc_in, back_out, give_out, *refs = refs
        bg_outs, (acc, *refs) = refs[:5], refs[5:]
    b32, s_ref, kf, vf, kq, vq, kqt, vqt, dk, dv = refs
    yh, x, yl, core = place_ref[0], place_ref[1], place_ref[2], place_ref[4]
    low = lax.broadcasted_iota(jnp.int32, (32, 128), 1) < 64
    lens = [chain_ref[n] for n in range(CHAINS)]
    starts = [0, lens[0], lens[0] + lens[1], lens[0] + lens[1] + lens[2]]

    def pick(values, n):
        return jnp.where(
            n < 2, jnp.where(n == 0, values[0], values[1]), jnp.where(n == 2, values[2], values[3])
        )

    def place_of(t):
        return pick(starts, t // 8) + (t % 8) * TOK

    def bias_piece(a, b, c, n):
        here, left, right, far_0, far_1 = bias_refs
        if a == 2:
            return (far_1 if b else far_0)[c, n]
        return {0: here, 1: left, 3: right}[a][2 * b + c, n]

    def bias_grad_place(a, b):
        here, first_right, first_left, then_right, then_left = bg_outs
        return {
            (0, 0): (here, 0),
            (0, 1): (here, 2),
            (1, 0): (first_left, 0),
            (1, 1): (then_left, 0),
            (2, 0): (first_right, 0),
            (2, 1): (first_left, 2),
            (3, 0): (then_right, 0),
            (3, 1): (first_right, 2),
        }[a, b]

    def build(t, _):
        at = place_of(t)
        yls, n = (t // 16) ^ yl, t % 16
        for m in range(4):
            xs = 2 * (m % 2)
            left = bias_piece(xs, m // 2, yls, n).astype(F32) * LOG2E
            right = bias_piece(xs + 1, m // 2, yls, n).astype(F32) * LOG2E
            b32[m, pl.ds(at, 32), :] = jnp.where(low, left, swap_halves(right))
            b32[m, pl.ds(at + 32, 32), :] = jnp.where(low, swap_halves(left), right)
        mine = recv_ref[t, :TOK, :].astype(F32)
        theirs = other_ref[t].astype(F32)
        kf[pl.ds(at, TOK), :] = jnp.where(core == 0, mine, theirs)
        vf[pl.ds(at, TOK), :] = jnp.where(core == 0, theirs, mine)
        return 0

    lax.fori_loop(0, COLS, build, 0, unroll=8)
    acc[:, :KEYS, :] = jnp.zeros((4, KEYS, 128), F32) if first else acc_in[...]
    keys = kf[:KEYS, :].astype(BF16)
    values = vf[:KEYS, :].astype(BF16)
    kq[...] = keys
    vq[...] = values
    kqt[...] = keys.T
    vqt[...] = values.T

    homes = [((yh ^ (p // 4)) * 4 + ((x - p % 4) & 3)) * 4 for p in range(ROWS)]

    def queries(lo):
        return jnp.concatenate(
            [recv_ref[pl.ds(at, 4), lo : lo + SUB, :].reshape(TOK, 128) for at in homes], axis=0
        )

    query = queries(TOK)
    cot = queries(TOK + SUB)
    query_t = query.T
    cot_t = cot.T
    lanes = lane_group((QRY, 128))
    subs = lax.broadcasted_iota(jnp.int32, (128, QRY), 0) // D
    zero = jnp.zeros((), BF16)
    chunks = [slice(c * CHUNK, (c + 1) * CHUNK) for c in range(KEYS // CHUNK)]
    out_t, dq_t = [], []
    for i in range(QUAD):
        band = slice(i * D, (i + 1) * D)
        q_m = jnp.where(lanes == i, query, zero)
        c_m = jnp.where(lanes == i, cot, zero)
        qt_m = jnp.where(subs == i, query_t, zero)
        ct_m = jnp.where(subs == i, cot_t, zero)
        top = jnp.full((8, QRY), -3e38, F32)
        for rows in chunks:
            s = nn(kq[rows, :], qt_m) * (SCALE * LOG2E)
            s = s + jnp.concatenate([b32[m, rows, :] for m in range(4)], axis=1)
            s_ref[rows, :] = s
            top = jnp.maximum(top, jnp.max(s.reshape(CHUNK // 8, 8, QRY), axis=0))
        top = jnp.max(top, axis=0, keepdims=True)
        total = jnp.zeros((8, QRY), F32)
        out = jnp.zeros((D, QRY), F32)
        for rows in chunks:
            e = jnp.exp2(s_ref[rows, :] - top)
            s_ref[rows, :] = e
            total = total + jnp.sum(e.reshape(CHUNK // 8, 8, QRY), axis=0)
            out = out + nn(vqt[band, rows], e.astype(BF16))
        inv = 1.0 / jnp.sum(total, axis=0, keepdims=True)
        out = out * inv
        delta = jnp.sum(cot_t[band].astype(F32) * out, axis=0, keepdims=True)
        dq = jnp.zeros((D, QRY), F32)
        for rows in chunks:
            prob = s_ref[rows, :] * inv
            ds = prob * (nn(vq[rows, :], ct_m) - delta)
            for m in range(4):
                acc[m, rows, :] += ds[:, m * 128 : (m + 1) * 128]
            half = ds.astype(BF16)
            key_part = nn(half, q_m)
            value_part = nn(prob.astype(BF16), c_m)
            if i:
                dk[rows, :] += key_part
                dv[rows, :] += value_part
            else:
                dk[rows, :] = key_part
                dv[rows, :] = value_part
            dq = dq + nn(kqt[band, rows], half)
        out_t.append(out)
        dq_t.append(dq * SCALE)
    dq = jnp.concatenate(dq_t, axis=0).T.astype(BF16)
    out = jnp.concatenate(out_t, axis=0).T.astype(BF16)
    for p, at in enumerate(homes):
        part = slice(p * TOK, (p + 1) * TOK)
        back_out[pl.ds(at, 4), TOK : TOK + SUB, :] = dq[part].reshape(4, SUB, 128)
        back_out[pl.ds(at, 4), TOK + SUB :, :] = out[part].reshape(4, SUB, 128)

    def spread(t, _):
        at = place_of(t)
        here = lax.broadcasted_iota(jnp.int32, (TOK, 128), 0) < pick(lens, t // 8) - (t % 8) * TOK
        key_grad = jnp.where(here, dk[pl.ds(at, TOK), :] * SCALE, 0.0).astype(BF16)
        value_grad = jnp.where(here, dv[pl.ds(at, TOK), :], 0.0).astype(BF16)
        back_out[t, :TOK, :] = jnp.where(core == 0, key_grad, value_grad)
        give_out[t] = jnp.where(core == 0, value_grad, key_grad)
        if first:
            return 0
        yls, n = (t // 16) ^ yl, t % 16
        for m in range(4):
            xs = 2 * (m % 2)
            top = jnp.where(here[:32], acc[m, pl.ds(at, 32), :], 0.0)
            bottom = jnp.where(here[32:], acc[m, pl.ds(at + 32, 32), :], 0.0)
            left = jnp.where(low, top, swap_halves(bottom))
            right = jnp.where(low, swap_halves(top), bottom)
            for a, value in ((xs, left), (xs + 1, right)):
                ref, base = bias_grad_place(a, m // 2)
                ref[base + yls, n] = value.astype(BF16)
        return 0

    lax.fori_loop(0, COLS, spread, 0, unroll=8)


def merge_kernel(back_ref, given_ref, out_ref):
    own = back_ref[:, :TOK, :].astype(F32)
    out_ref[:, :TOK, :] = (own + given_ref[...].astype(F32)).astype(BF16)
    out_ref[:, TOK:, :] = back_ref[:, TOK:, :]


def merge(back, given):
    return call(merge_kernel, [whole()] * 2, shape((COLS, CHUNK_ROWS, 128)), moved=2_000_000)(
        back, given
    )


def finish_kernel(part, recv_ref, gates_ref, ograd_ref, pair_ref, grad_ref, wp_ref, *refs):
    if part:
        weight_in, *bias_refs, pair_out, send_out, pg, gt, weight_out = refs
    else:
        pair_out, weight_out, pg, gt = refs
    quads = [2 * part, 2 * part + 1]
    for n, q in enumerate(quads):
        rows = slice(n * TOK, (n + 1) * TOK)
        for h in range(H):
            base = n * 16 + h * 4
            key = recv_ref[base, :TOK].astype(F32) + recv_ref[base + 2, :TOK].astype(F32)
            value = recv_ref[base + 1, :TOK].astype(F32) + recv_ref[base + 3, :TOK].astype(F32)
            query = jnp.concatenate(
                [recv_ref[base + j, TOK : TOK + SUB] for j in range(4)], axis=0
            )
            out = jnp.concatenate(
                [recv_ref[base + j, TOK + SUB :] for j in range(4)], axis=0
            ).astype(F32)
            lanes = slice(h * 128, (h + 1) * 128)
            sig = jax.nn.sigmoid(gates_ref[q, :, lanes].astype(F32))
            og = ograd_ref[q, :, lanes].astype(F32)
            gt[rows, lanes] = (sig * out).astype(BF16)
            pg[rows, h * 512 : h * 512 + 128] = query
            pg[rows, h * 512 + 128 : h * 512 + 256] = key.astype(BF16)
            pg[rows, h * 512 + 256 : h * 512 + 384] = value.astype(BF16)
            pg[rows, h * 512 + 384 : h * 512 + 512] = (og * out * sig * (1.0 - sig)).astype(BF16)
    wp = wp_ref[...]
    group = lane_group(wp.shape)
    zero = jnp.zeros((), BF16)
    grads = pg[...]
    gated = gt[...]
    for r in range(QUAD):
        pair_grad = nt(grads, jnp.where(group == r, wp, zero)).astype(BF16)
        for n in range(2):
            pair_out[4 * n + r] = pair_grad[n * TOK : (n + 1) * TOK]
    turned = grads.T
    gated_t = gated.T
    for r in range(QUAD):
        pair_r = jnp.concatenate([pair_ref[4 * q + r] for q in quads], axis=0)
        grad_r = jnp.concatenate([grad_ref[4 * q + r] for q in quads], axis=0)
        proj_part = nn(turned, pair_r)
        out_part = nn(gated_t, grad_r)
        for n in range(20):
            at = (n % 16) * 128 + r * D
            piece = (proj_part if n < 16 else out_part)[at : at + D] * (1.0 / LEN)
            rows = slice(n * D, (n + 1) * D)
            if r:
                weight_out[rows] += piece
            elif part:
                weight_out[rows] = weight_in[rows] + piece
            else:
                weight_out[rows] = piece
    if not part:
        return
    weight_out[640:] = jnp.zeros((128, 128), F32)
    bias_sum = bias_refs[0][...].astype(F32)
    for ref in bias_refs[1:]:
        bias_sum = bias_sum + ref[...].astype(F32)
    send_out[:, :32, :] = bias_sum.astype(BF16)
    send_out[:, 32:, :] = weight_out[...].astype(BF16).reshape(16, 48, 128)


def finish(part, home, gates, ograd, pair_rep, grad_out, wp, *more):
    last = shape((16, 80, 128)) if part else shape((640, 128), F32)
    scratch = [pltpu.VMEM((128, 2048), BF16), pltpu.VMEM((128, 512), BF16)]
    if part:
        scratch.append(pltpu.VMEM((768, 128), F32))
    return call(
        lambda *refs: finish_kernel(part, *refs),
        [whole()] * (6 + len(more)),
        (shape((8, TOK, 128)), last),
        scratch,
        flops=1_000_000_000,
        moved=3_000_000,
    )(home, gates, ograd, pair_rep, grad_out, wp, *more)


def whole():
    return pl.BlockSpec(memory_space=pltpu.VMEM)


def scalar():
    return pl.BlockSpec(memory_space=pltpu.SMEM)


def call(kernel, in_specs, outs, scratch=(), flops=0, moved=0):
    return pl.pallas_call(
        kernel,
        out_shape=outs,
        in_specs=in_specs,
        out_specs=jax.tree.map(lambda _: whole(), outs),
        scratch_shapes=list(scratch),
        compiler_params=pltpu.CompilerParams(vmem_limit_bytes=VMEM_LIMIT),
        cost_estimate=pl.CostEstimate(flops=flops, bytes_accessed=moved, transcendentals=0),
    )


def shape(dims, dtype=BF16):
    return jax.ShapeDtypeStruct(dims, dtype)


def query_order():
    perm = np.zeros((256, 256), np.float32)
    for s in range(4):
        for j in range(4):
            for t in range(SUB):
                perm[s * 64 + j * SUB + t, j * 64 + s * SUB + t] = 1.0
    return perm


def widen(groups):
    source = lax.broadcasted_iota(jnp.int32, (groups * D, groups * 128), 0)
    target = lax.broadcasted_iota(jnp.int32, (groups * D, groups * 128), 1)
    same = (source // D == target // 128) & (source % D == target % D)
    return same.astype(BF16)


def shift(x, axis, step):
    count = {"x": 4, "c": 2}[axis]
    return lax.ppermute(x, axis, [(n, (n + step) % count) for n in range(count)])


def flip_y(x, bits):
    return lax.ppermute(x, ("yh", "yl"), [(n, n ^ bits) for n in range(4)])


PIECE = (32, 128)
HALF = (2, 16) + PIECE
FULL = (4, 16) + PIECE


def gather_bias(own):
    here = jnp.stack([own] + [flip_y(own, bits) for bits in range(1, 4)])
    left = shift(here, "x", 1)
    right = shift(here, "x", -1)
    return here, left, right, shift(right[:2], "x", -1), shift(left[2:], "x", 1)


def total(*terms):
    return sum(t.astype(F32) for t in terms).astype(BF16)


def scatter_bias(parts):
    here, first_right, first_left, then_right, then_left = parts
    from_left = shift(first_right, "x", 1)
    from_right = shift(first_left, "x", -1)
    from_left_a = shift(total(then_right, from_left[:2]), "x", 1)
    from_right_b = shift(total(then_left, from_right[2:]), "x", -1)
    sum_a = total(here[:2], from_left_a, from_right[:2])
    sum_b = total(here[2:], from_right_b, from_left[2:])
    return sum_a[0], flip_y(sum_a[1], 1), flip_y(sum_b[0], 2), flip_y(sum_b[1], 3)


CHUNK_ROWS = TOK + 2 * SUB


def attend_call(first, place, chain_lengths, recv, other, bias, acc):
    packed = pltpu.VMEM((4, LEN, 128), F32)
    tall = [pltpu.VMEM((LEN, 128), F32)] * 2
    scratch = [packed, pltpu.VMEM((KEYS, QRY), F32)] + tall
    scratch += [pltpu.VMEM((KEYS, 128), BF16)] * 2 + [pltpu.VMEM((128, KEYS), BF16)] * 2 + tall
    outs = (shape((COLS, CHUNK_ROWS, 128)), shape((COLS, TOK, 128)))
    if first:
        outs += (shape((4, KEYS, 128), F32),)
    else:
        outs += (shape(FULL),) * 3 + (shape(HALF),) * 2
        scratch = [packed] + scratch
    return call(
        lambda *refs: attend_kernel(first, *refs),
        [scalar()] * 2 + [whole()] * (7 + len(acc)),
        outs,
        scratch,
        flops=25_000_000_000,
        moved=10_000_000,
    )(place, chain_lengths, recv, other, *bias, *acc)


def attend(first, place, chain_lengths, recv, bias, acc=()):
    other = shift(recv[:, :TOK], "c", 1)
    back, give, *rest = attend_call(first, place, chain_lengths, recv, other, bias, acc)
    given = shift(give, "c", 1)
    merged = merge(back, given)
    return merged, rest


def on_device(pair_rep, w_proj, bias_logits, chain_lengths, w_out, grad_out):
    col = ("yl", "z", "c")
    plane = ("yh", "x", "yl")
    line = ("z", "c")
    place = jnp.stack([lax.axis_index(a) for a in ("yh", "x", "yl", "z", "c")]).astype(jnp.int32)
    perm = jnp.asarray(query_order(), BF16)

    packed = call(
        bias_pack_kernel, [scalar(), scalar(), whole(), whole()], shape((16,) + PIECE)
    )(place, chain_lengths, perm, jnp.swapaxes(bias_logits, 1, 2))
    bias = gather_bias(lax.all_to_all(packed, line, 0, 0, tiled=True))
    wp = jnp.dot(w_proj, widen(16), preferred_element_type=F32).astype(BF16)
    wo = jnp.dot(w_out.T, widen(4), preferred_element_type=F32).astype(BF16)
    part = shape((COLS, CHUNK_ROWS, 128))
    send_a, send_b, gates, ograd = call(
        project_kernel,
        [whole()] * 4,
        (part, part, shape((4, TOK, 512)), shape((4, TOK, 512))),
        flops=700_000_000,
        moved=6_000_000,
    )(pair_rep, grad_out, wp, wo)
    recv_a = lax.all_to_all(send_a, col, 0, 0, tiled=True)
    recv_b = lax.all_to_all(send_b, col, 0, 0, tiled=True)
    back_a, acc = attend(True, place, chain_lengths, recv_a, bias)
    home_a = lax.all_to_all(back_a, col, 0, 0, tiled=True)
    back_b, bg = attend(False, place, chain_lengths, recv_b, bias, acc)
    home_b = lax.all_to_all(back_b, col, 0, 0, tiled=True)
    shared = (gates, ograd, pair_rep, grad_out, wp)
    pair_a, weights = finish(0, home_a, *shared)
    pair_b, pieces = finish(1, home_b, *shared, weights, *scatter_bias(bg))
    pair_grad = jnp.concatenate([pair_a, pair_b], axis=0)
    pieces = lax.all_to_all(pieces, line, 0, 0, tiled=True)
    bias_grad = call(bias_unpack_kernel, [whole()] * 2, shape((H, TOK, 256), F32))(perm, pieces)
    share = jnp.sum(pieces[:, 32:].astype(F32), axis=0)
    share = lax.all_to_all(
        jnp.broadcast_to(share.astype(BF16)[None], (16, 48, 128)), plane, 0, 0, tiled=True
    )
    share = jnp.sum(share.astype(F32), axis=0).astype(BF16)
    every = lax.all_to_all(
        jnp.broadcast_to(share[None], (16, 48, 128)), line, 0, 0, tiled=True
    )
    every = every.reshape(768, 128).astype(F32)
    return (pair_grad, jnp.swapaxes(bias_grad, 1, 2), every[:512].T, every[512:640])


def solution(mesh):
    fine = Mesh(mesh.devices.reshape(2, 4, 2, 8, 2), ("yh", "x", "yl", "z", "c"))
    row = ("yh", "x")
    col = ("yl", "z", "c")
    return jax.shard_map(
        on_device,
        mesh=fine,
        in_specs=(
            P(row, col, None),
            P(),
            P(None, row, col),
            P(),
            P(),
            P(row, col, None),
        ),
        out_specs=(P(row, col, None), P(None, row, col), P(), P()),
        check_vma=False,
    )
```

```python
import functools

import jax
import jax.numpy as jnp
import numpy as np
from jax import lax
from jax.experimental import pallas as pl
from jax.experimental.pallas import tpu as pltpu
from jax.sharding import Mesh
from jax.sharding import PartitionSpec as P

H = 4
D = 32
CHAINS = 4
NEG_BIG = -1e30
LOG2E = 1.4426950408889634
SCALE = D ** (-0.5)
F32 = jnp.float32
BF16 = jnp.bfloat16
QUAD = 4
TOK = 64
SUB = 16
COLS = 32
ROWS = 8
LEN = TOK * COLS
QRY = SUB * COLS
VMEM_LIMIT = 56 * 1024 * 1024


def dot(a, b, dims):
    return lax.dot_general(a, b, (dims, ((), ())), preferred_element_type=F32)


def nn(a, b):
    return dot(a, b, ((1,), (0,)))


def nt(a, b):
    return dot(a, b, ((1,), (1,)))


def tn(a, b):
    return dot(a, b, ((0,), (0,)))


def lane_group(shape):
    return (lax.broadcasted_iota(jnp.int32, shape, 1) // D) % QUAD


def swap_halves(x):
    return jnp.concatenate([x[:, TOK:], x[:, :TOK]], axis=1)


def bias_pack_kernel(place_ref, chain_ref, perm_ref, bias_ref, out_ref):
    block = (place_ref[2] * 8 + place_ref[3]) * 2 + place_ref[4]
    per_chain = COLS // CHAINS
    limit = chain_ref[block // per_chain] - (block % per_chain) * TOK
    low = lax.broadcasted_iota(jnp.int32, (32, 128), 1) < 64
    valid = lax.broadcasted_iota(jnp.int32, (TOK, 256), 0) < limit
    for h in range(H):
        ordered = jnp.where(valid, nn(bias_ref[h], perm_ref[...]), NEG_BIG)
        for m in range(2):
            top = ordered[:32, m * 128 : (m + 1) * 128]
            bottom = ordered[32:, m * 128 : (m + 1) * 128]
            out_ref[h * 4 + 2 * m] = jnp.where(low, top, swap_halves(bottom)).astype(BF16)
            out_ref[h * 4 + 2 * m + 1] = jnp.where(low, swap_halves(top), bottom).astype(BF16)


def bias_unpack_kernel(perm_ref, parts_ref, out_ref):
    low = lax.broadcasted_iota(jnp.int32, (32, 128), 1) < 64
    for h in range(H):
        tops, bottoms = [], []
        for m in range(2):
            first = parts_ref[h * 4 + 2 * m, :32].astype(F32)
            second = parts_ref[h * 4 + 2 * m + 1, :32].astype(F32)
            tops.append(jnp.where(low, first, swap_halves(second)))
            bottoms.append(jnp.where(low, swap_halves(first), second))
        ordered = jnp.concatenate(
            [jnp.concatenate(tops, axis=1), jnp.concatenate(bottoms, axis=1)], axis=0
        ).astype(BF16)
        out_ref[h] = nt(ordered, perm_ref[...])


def project_kernel(
    pair_ref, grad_ref, wp_ref, wo_ref, send_a_ref, send_b_ref, gates_ref, ograd_ref
):
    wp = wp_ref[...]
    wo = wo_ref[...]
    group_p = lane_group(wp.shape)
    group_o = lane_group(wo.shape)
    zero = jnp.zeros((), BF16)
    wide_p = jnp.concatenate([jnp.where(group_p == r, wp, zero) for r in range(QUAD)], axis=0)
    wide_o = jnp.concatenate([jnp.where(group_o == r, wo, zero) for r in range(QUAD)], axis=0)

    def quads(ref):
        return jnp.concatenate(
            [
                jnp.concatenate([ref[4 * q + r] for r in range(QUAD)], axis=1)
                for q in range(4)
            ],
            axis=0,
        )

    proj = nn(quads(pair_ref), wide_p).astype(BF16)
    ograd = nn(quads(grad_ref), wide_o).astype(BF16)
    for q in range(4):
        rows = slice(q * TOK, (q + 1) * TOK)
        send_ref = send_b_ref if q // 2 else send_a_ref
        for h in range(H):
            query, key, value, gate = [
                proj[rows, h * 512 + p * 128 : h * 512 + (p + 1) * 128] for p in range(4)
            ]
            og = ograd[rows, h * 128 : (h + 1) * 128]
            gates_ref[q, :, h * 128 : (h + 1) * 128] = gate
            ograd_ref[q, :, h * 128 : (h + 1) * 128] = og
            cot = (og.astype(F32) * jax.nn.sigmoid(gate.astype(F32))).astype(BF16)
            for j in range(4):
                dest = (q % 2) * 16 + h * 4 + j
                send_ref[dest, :TOK] = value if j % 2 else key
                part = slice(j * SUB, (j + 1) * SUB)
                send_ref[dest, TOK : TOK + SUB] = query[part]
                send_ref[dest, TOK + SUB :] = cot[part]


CHUNK = 512
KEYS = 3 * LEN // 4


def attend_kernel(first, place_ref, chain_ref, recv_ref, other_ref, *refs):
    bias_refs, refs = refs[:8], refs[8:]
    if first:
        back_out, give_out, acc, *refs = refs
    else:
        acc_in, back_out, give_out, *refs = refs
        bg_outs, (acc, *refs) = refs[:5], refs[5:]
    b32, s_ref, kf, vf, kq, vq, kqt, vqt, dk, dv = refs
    yh, x, yl, core = place_ref[0], place_ref[1], place_ref[2], place_ref[4]
    low = lax.broadcasted_iota(jnp.int32, (32, 128), 1) < 64
    lens = [chain_ref[n] for n in range(CHAINS)]
    starts = [0, lens[0], lens[0] + lens[1], lens[0] + lens[1] + lens[2]]

    def place_of(chain, n):
        return starts[chain] + n * TOK

    def bias_piece(chain, a, b, c, n):
        if chain % 2:
            return bias_refs[4 + a][2 * b + c, n]
        return bias_refs[2 * b + c][a, n]

    def bias_grad_place(a, b):
        here, first_right, first_left, then_right, then_left = bg_outs
        return {
            (0, 0): (here, 0),
            (0, 1): (here, 2),
            (1, 0): (first_left, 0),
            (1, 1): (then_left, 0),
            (2, 0): (first_right, 0),
            (2, 1): (first_left, 2),
            (3, 0): (then_right, 0),
            (3, 1): (first_right, 2),
        }[a, b]

    def each_chain(body):
        for own in range(2):

            @pl.when(yl == own)
            def _(own=own):
                for chain in range(CHAINS):
                    step = functools.partial(body, chain, (chain // 2) ^ own)
                    lax.fori_loop(0, 8, step, 0, unroll=True)

    def build(chain, c, n, _):
        at = place_of(chain, n)
        for m in range(4):
            xs = 2 * (m % 2)
            left = bias_piece(chain, xs, m // 2, c, n).astype(F32) * LOG2E
            right = bias_piece(chain, xs + 1, m // 2, c, n).astype(F32) * LOG2E
            b32[m, pl.ds(at, 32), :] = jnp.where(low, left, swap_halves(right))
            b32[m, pl.ds(at + 32, 32), :] = jnp.where(low, swap_halves(left), right)
        t = chain * 8 + n
        mine = recv_ref[t, :TOK, :].astype(F32)
        theirs = other_ref[t].astype(F32)
        kf[pl.ds(at, TOK), :] = jnp.where(core == 0, mine, theirs)
        vf[pl.ds(at, TOK), :] = jnp.where(core == 0, theirs, mine)
        return 0

    each_chain(build)
    acc[:, :KEYS, :] = jnp.zeros((4, KEYS, 128), F32) if first else acc_in[...]
    keys = kf[:KEYS, :].astype(BF16)
    values = vf[:KEYS, :].astype(BF16)
    kq[...] = keys
    vq[...] = values
    kqt[...] = keys.T
    vqt[...] = values.T

    homes = [((yh ^ (p // 4)) * 4 + ((x - p % 4) & 3)) * 4 for p in range(ROWS)]

    def queries(lo):
        return jnp.concatenate(
            [recv_ref[pl.ds(at, 4), lo : lo + SUB, :].reshape(TOK, 128) for at in homes], axis=0
        )

    query = queries(TOK)
    cot = queries(TOK + SUB)
    query_t = query.T
    cot_t = cot.T
    lanes = lane_group((QRY, 128))
    subs = lax.broadcasted_iota(jnp.int32, (128, QRY), 0) // D
    zero = jnp.zeros((), BF16)
    chunks = [slice(c * CHUNK, (c + 1) * CHUNK) for c in range(KEYS // CHUNK)]
    out_t, dq_t = [], []
    for i in range(QUAD):
        band = slice(i * D, (i + 1) * D)
        q_m = jnp.where(lanes == i, query, zero)
        c_m = jnp.where(lanes == i, cot, zero)
        qt_m = jnp.where(subs == i, query_t, zero)
        ct_m = jnp.where(subs == i, cot_t, zero)
        top = jnp.full((8, QRY), -3e38, F32)
        for rows in chunks:
            s = nn(kq[rows, :], qt_m) * (SCALE * LOG2E)
            s = s + jnp.concatenate([b32[m, rows, :] for m in range(4)], axis=1)
            s_ref[rows, :] = s
            top = jnp.maximum(top, jnp.max(s.reshape(CHUNK // 8, 8, QRY), axis=0))
        top = jnp.max(top, axis=0, keepdims=True)
        total = jnp.zeros((8, QRY), F32)
        out = jnp.zeros((D, QRY), F32)
        for rows in chunks:
            e = jnp.exp2(s_ref[rows, :] - top)
            s_ref[rows, :] = e
            total = total + jnp.sum(e.reshape(CHUNK // 8, 8, QRY), axis=0)
            out = out + nn(vqt[band, rows], e.astype(BF16))
        inv = 1.0 / jnp.sum(total, axis=0, keepdims=True)
        out = out * inv
        delta = jnp.sum(cot_t[band].astype(F32) * out, axis=0, keepdims=True)
        dq = jnp.zeros((D, QRY), F32)
        for rows in chunks:
            prob = s_ref[rows, :] * inv
            ds = prob * (nn(vq[rows, :], ct_m) - delta)
            for m in range(4):
                acc[m, rows, :] += ds[:, m * 128 : (m + 1) * 128]
            half = ds.astype(BF16)
            key_part = nn(half, q_m)
            value_part = nn(prob.astype(BF16), c_m)
            if i:
                dk[rows, :] += key_part
                dv[rows, :] += value_part
            else:
                dk[rows, :] = key_part
                dv[rows, :] = value_part
            dq = dq + nn(kqt[band, rows], half)
        out_t.append(out)
        dq_t.append(dq * SCALE)
    dq = jnp.concatenate(dq_t, axis=0).T.astype(BF16)
    out = jnp.concatenate(out_t, axis=0).T.astype(BF16)
    for p, at in enumerate(homes):
        part = slice(p * TOK, (p + 1) * TOK)
        back_out[pl.ds(at, 4), TOK : TOK + SUB, :] = dq[part].reshape(4, SUB, 128)
        back_out[pl.ds(at, 4), TOK + SUB :, :] = out[part].reshape(4, SUB, 128)

    def spread(chain, c, n, _):
        at = place_of(chain, n)
        here = lax.broadcasted_iota(jnp.int32, (TOK, 128), 0) < lens[chain] - n * TOK
        key_grad = jnp.where(here, dk[pl.ds(at, TOK), :] * SCALE, 0.0).astype(BF16)
        value_grad = jnp.where(here, dv[pl.ds(at, TOK), :], 0.0).astype(BF16)
        t = chain * 8 + n
        back_out[t, :TOK, :] = jnp.where(core == 0, key_grad, value_grad)
        give_out[t] = jnp.where(core == 0, value_grad, key_grad)
        if first:
            return 0
        for m in range(4):
            xs = 2 * (m % 2)
            top = jnp.where(here[:32], acc[m, pl.ds(at, 32), :], 0.0)
            bottom = jnp.where(here[32:], acc[m, pl.ds(at + 32, 32), :], 0.0)
            left = jnp.where(low, top, swap_halves(bottom))
            right = jnp.where(low, swap_halves(top), bottom)
            for a, value in ((xs, left), (xs + 1, right)):
                ref, base = bias_grad_place(a, m // 2)
                ref[base + c, (chain % 2) * 8 + n] = value.astype(BF16)
        return 0

    each_chain(spread)


def merge_kernel(back_ref, given_ref, out_ref):
    own = back_ref[:, :TOK, :].astype(F32)
    out_ref[:, :TOK, :] = (own + given_ref[...].astype(F32)).astype(BF16)
    out_ref[:, TOK:, :] = back_ref[:, TOK:, :]


def merge(back, given):
    return call(merge_kernel, [whole()] * 2, shape((COLS, CHUNK_ROWS, 128)), moved=2_000_000)(
        back, given
    )


def finish_kernel(part, recv_ref, gates_ref, ograd_ref, pair_ref, grad_ref, wp_ref, *refs):
    if part:
        weight_in, *bias_refs, pair_out, send_out, pg, gt, weight_out = refs
    else:
        pair_out, weight_out, pg, gt = refs
    quads = [2 * part, 2 * part + 1]
    for n, q in enumerate(quads):
        rows = slice(n * TOK, (n + 1) * TOK)
        for h in range(H):
            base = n * 16 + h * 4
            key = recv_ref[base, :TOK].astype(F32) + recv_ref[base + 2, :TOK].astype(F32)
            value = recv_ref[base + 1, :TOK].astype(F32) + recv_ref[base + 3, :TOK].astype(F32)
            query = jnp.concatenate(
                [recv_ref[base + j, TOK : TOK + SUB] for j in range(4)], axis=0
            )
            out = jnp.concatenate(
                [recv_ref[base + j, TOK + SUB :] for j in range(4)], axis=0
            ).astype(F32)
            lanes = slice(h * 128, (h + 1) * 128)
            sig = jax.nn.sigmoid(gates_ref[q, :, lanes].astype(F32))
            og = ograd_ref[q, :, lanes].astype(F32)
            gt[rows, lanes] = (sig * out).astype(BF16)
            pg[rows, h * 512 : h * 512 + 128] = query
            pg[rows, h * 512 + 128 : h * 512 + 256] = key.astype(BF16)
            pg[rows, h * 512 + 256 : h * 512 + 384] = value.astype(BF16)
            pg[rows, h * 512 + 384 : h * 512 + 512] = (og * out * sig * (1.0 - sig)).astype(BF16)
    wp = wp_ref[...]
    group = lane_group(wp.shape)
    zero = jnp.zeros((), BF16)
    grads = pg[...]
    gated = gt[...]
    for r in range(QUAD):
        pair_grad = nt(grads, jnp.where(group == r, wp, zero)).astype(BF16)
        for n in range(2):
            pair_out[4 * n + r] = pair_grad[n * TOK : (n + 1) * TOK]
    turned = grads.T
    gated_t = gated.T
    for r in range(QUAD):
        pair_r = jnp.concatenate([pair_ref[4 * q + r] for q in quads], axis=0)
        grad_r = jnp.concatenate([grad_ref[4 * q + r] for q in quads], axis=0)
        proj_part = nn(turned, pair_r)
        out_part = nn(gated_t, grad_r)
        for n in range(20):
            at = (n % 16) * 128 + r * D
            piece = (proj_part if n < 16 else out_part)[at : at + D] * (1.0 / LEN)
            rows = slice(n * D, (n + 1) * D)
            if r:
                weight_out[rows] += piece
            elif part:
                weight_out[rows] = weight_in[rows] + piece
            else:
                weight_out[rows] = piece
    if not part:
        return
    weight_out[640:] = jnp.zeros((128, 128), F32)
    bias_sum = bias_refs[0][...].astype(F32)
    for ref in bias_refs[1:]:
        bias_sum = bias_sum + ref[...].astype(F32)
    send_out[:, :32, :] = bias_sum.astype(BF16)
    send_out[:, 32:, :] = weight_out[...].astype(BF16).reshape(16, 48, 128)


def finish(part, home, gates, ograd, pair_rep, grad_out, wp, *more):
    last = shape((16, 80, 128)) if part else shape((640, 128), F32)
    scratch = [pltpu.VMEM((128, 2048), BF16), pltpu.VMEM((128, 512), BF16)]
    if part:
        scratch.append(pltpu.VMEM((768, 128), F32))
    return call(
        lambda *refs: finish_kernel(part, *refs),
        [whole()] * (6 + len(more)),
        (shape((8, TOK, 128)), last),
        scratch,
        flops=1_000_000_000,
        moved=3_000_000,
    )(home, gates, ograd, pair_rep, grad_out, wp, *more)


def whole():
    return pl.BlockSpec(memory_space=pltpu.VMEM)


def scalar():
    return pl.BlockSpec(memory_space=pltpu.SMEM)


def call(kernel, in_specs, outs, scratch=(), flops=0, moved=0):
    return pl.pallas_call(
        kernel,
        out_shape=outs,
        in_specs=in_specs,
        out_specs=jax.tree.map(lambda _: whole(), outs),
        scratch_shapes=list(scratch),
        compiler_params=pltpu.CompilerParams(vmem_limit_bytes=VMEM_LIMIT),
        cost_estimate=pl.CostEstimate(flops=flops, bytes_accessed=moved, transcendentals=0),
    )


def shape(dims, dtype=BF16):
    return jax.ShapeDtypeStruct(dims, dtype)


def query_order():
    perm = np.zeros((256, 256), np.float32)
    for s in range(4):
        for j in range(4):
            for t in range(SUB):
                perm[s * 64 + j * SUB + t, j * 64 + s * SUB + t] = 1.0
    return perm


def widen(groups):
    source = lax.broadcasted_iota(jnp.int32, (groups * D, groups * 128), 0)
    target = lax.broadcasted_iota(jnp.int32, (groups * D, groups * 128), 1)
    same = (source // D == target // 128) & (source % D == target % D)
    return same.astype(BF16)


def shift(x, axis, step):
    count = {"x": 4, "c": 2}[axis]
    return lax.ppermute(x, axis, [(n, (n + step) % count) for n in range(count)])


def flip_y(x, bits):
    return lax.ppermute(x, ("yh", "yl"), [(n, n ^ bits) for n in range(4)])


PIECE = (32, 128)
HALF = (2, 16) + PIECE
FULL = (4, 16) + PIECE


def gather_bias(own):
    even, odd = own[:8], own[8:]
    even = jnp.stack([even] + [shift(even, "x", n) for n in range(1, 4)])
    odd = jnp.stack([odd] + [flip_y(odd, n) for n in range(1, 4)])
    first = (even, odd)
    even = [even] + [flip_y(even, n) for n in range(1, 4)]
    odd = [odd] + [shift(odd, "x", n) for n in range(1, 4)]
    return even + odd, first


def total(*terms):
    return sum(t.astype(F32) for t in terms).astype(BF16)


def scatter_bias(parts):
    here, first_right, first_left, then_right, then_left = parts
    from_left = shift(first_right, "x", 1)
    from_right = shift(first_left, "x", -1)
    from_left_a = shift(total(then_right, from_left[:2]), "x", 1)
    from_right_b = shift(total(then_left, from_right[2:]), "x", -1)
    sum_a = total(here[:2], from_left_a, from_right[:2])
    sum_b = total(here[2:], from_right_b, from_left[2:])
    return sum_a[0], flip_y(sum_a[1], 1), flip_y(sum_b[0], 2), flip_y(sum_b[1], 3)


CHUNK_ROWS = TOK + 2 * SUB


def attend_call(first, place, chain_lengths, recv, other, bias, acc):
    packed = pltpu.VMEM((4, LEN, 128), F32)
    tall = [pltpu.VMEM((LEN, 128), F32)] * 2
    scratch = [packed, pltpu.VMEM((KEYS, QRY), F32)] + tall
    scratch += [pltpu.VMEM((KEYS, 128), BF16)] * 2 + [pltpu.VMEM((128, KEYS), BF16)] * 2 + tall
    outs = (shape((COLS, CHUNK_ROWS, 128)), shape((COLS, TOK, 128)))
    if first:
        outs += (shape((4, KEYS, 128), F32),)
    else:
        outs += (shape(FULL),) * 3 + (shape(HALF),) * 2
        scratch = [packed] + scratch
    return call(
        lambda *refs: attend_kernel(first, *refs),
        [scalar()] * 2 + [whole()] * (10 + len(acc)),
        outs,
        scratch,
        flops=25_000_000_000,
        moved=10_000_000,
    )(place, chain_lengths, recv, other, *bias, *acc)


def attend(first, place, chain_lengths, recv, bias, acc=()):
    other = shift(recv[:, :TOK], "c", 1)
    back, give, *rest = attend_call(first, place, chain_lengths, recv, other, bias, acc)
    given = shift(give, "c", 1)
    merged = merge(back, given)
    return merged, rest


def on_device(pair_rep, w_proj, bias_logits, chain_lengths, w_out, grad_out):
    col = ("yl", "z", "c")
    plane = ("yh", "x", "yl")
    line = ("z", "c")
    place = jnp.stack([lax.axis_index(a) for a in ("yh", "x", "yl", "z", "c")]).astype(jnp.int32)
    perm = jnp.asarray(query_order(), BF16)

    packed = call(
        bias_pack_kernel, [scalar(), scalar(), whole(), whole()], shape((16,) + PIECE)
    )(place, chain_lengths, perm, jnp.swapaxes(bias_logits, 1, 2))
    bias, first = gather_bias(lax.all_to_all(packed, line, 0, 0, tiled=True))
    wp = jnp.dot(w_proj, widen(16), preferred_element_type=F32).astype(BF16)
    wo = jnp.dot(w_out.T, widen(4), preferred_element_type=F32).astype(BF16)
    part = shape((COLS, CHUNK_ROWS, 128))
    send_a, send_b, gates, ograd = call(
        project_kernel,
        [whole()] * 4,
        (part, part, shape((4, TOK, 512)), shape((4, TOK, 512))),
        flops=700_000_000,
        moved=6_000_000,
    )(pair_rep, grad_out, wp, wo)
    recv_a = lax.all_to_all(send_a, col, 0, 0, tiled=True)
    recv_b = lax.all_to_all(send_b, col, 0, 0, tiled=True)
    recv_a, *first = lax.optimization_barrier((recv_a, *first))
    back_a, acc = attend(True, place, chain_lengths, recv_a, bias)
    home_a = lax.all_to_all(back_a, col, 0, 0, tiled=True)
    back_b, bg = attend(False, place, chain_lengths, recv_b, bias, acc)
    home_b = lax.all_to_all(back_b, col, 0, 0, tiled=True)
    shared = (gates, ograd, pair_rep, grad_out, wp)
    pair_a, weights = finish(0, home_a, *shared)
    pair_b, pieces = finish(1, home_b, *shared, weights, *scatter_bias(bg))
    pair_grad = jnp.concatenate([pair_a, pair_b], axis=0)
    pieces = lax.all_to_all(pieces, line, 0, 0, tiled=True)
    bias_grad = call(bias_unpack_kernel, [whole()] * 2, shape((H, TOK, 256), F32))(perm, pieces)
    share = jnp.sum(pieces[:, 32:].astype(F32), axis=0)
    share = lax.all_to_all(
        jnp.broadcast_to(share.astype(BF16)[None], (16, 48, 128)), plane, 0, 0, tiled=True
    )
    share = jnp.sum(share.astype(F32), axis=0).astype(BF16)
    every = lax.all_to_all(
        jnp.broadcast_to(share[None], (16, 48, 128)), line, 0, 0, tiled=True
    )
    every = every.reshape(768, 128).astype(F32)
    return (pair_grad, jnp.swapaxes(bias_grad, 1, 2), every[:512].T, every[512:640])


def solution(mesh):
    fine = Mesh(mesh.devices.reshape(2, 4, 2, 8, 2), ("yh", "x", "yl", "z", "c"))
    row = ("yh", "x")
    col = ("yl", "z", "c")
    return jax.shard_map(
        on_device,
        mesh=fine,
        in_specs=(
            P(row, col, None),
            P(),
            P(None, row, col),
            P(),
            P(),
            P(row, col, None),
        ),
        out_specs=(P(row, col, None), P(None, row, col), P(), P()),
        check_vma=False,
    )
```

```python
import functools

import jax
import jax.numpy as jnp
import numpy as np
from jax import lax
from jax.experimental import pallas as pl
from jax.experimental.pallas import tpu as pltpu
from jax.sharding import Mesh
from jax.sharding import PartitionSpec as P

H = 4
D = 32
CHAINS = 4
NEG_BIG = -1e30
LOG2E = 1.4426950408889634
SCALE = D ** (-0.5)
F32 = jnp.float32
BF16 = jnp.bfloat16
QUAD = 4
TOK = 64
SUB = 16
COLS = 32
ROWS = 8
LEN = TOK * COLS
QRY = SUB * COLS
VMEM_LIMIT = 56 * 1024 * 1024


def dot(a, b, dims):
    return lax.dot_general(a, b, (dims, ((), ())), preferred_element_type=F32)


def nn(a, b):
    return dot(a, b, ((1,), (0,)))


def nt(a, b):
    return dot(a, b, ((1,), (1,)))


def tn(a, b):
    return dot(a, b, ((0,), (0,)))


def lane_group(shape):
    return (lax.broadcasted_iota(jnp.int32, shape, 1) // D) % QUAD


def swap_halves(x):
    return jnp.concatenate([x[:, TOK:], x[:, :TOK]], axis=1)


def bias_pack_kernel(place_ref, chain_ref, perm_ref, bias_ref, out_ref):
    block = (place_ref[2] * 8 + place_ref[3]) * 2 + place_ref[4]
    per_chain = COLS // CHAINS
    limit = chain_ref[block // per_chain] - (block % per_chain) * TOK
    low = lax.broadcasted_iota(jnp.int32, (32, 128), 1) < 64
    valid = lax.broadcasted_iota(jnp.int32, (TOK, 256), 0) < limit
    for h in range(H):
        ordered = jnp.where(valid, nn(bias_ref[h], perm_ref[...]), NEG_BIG)
        for m in range(2):
            top = ordered[:32, m * 128 : (m + 1) * 128]
            bottom = ordered[32:, m * 128 : (m + 1) * 128]
            out_ref[h * 4 + 2 * m] = jnp.where(low, top, swap_halves(bottom)).astype(BF16)
            out_ref[h * 4 + 2 * m + 1] = jnp.where(low, swap_halves(top), bottom).astype(BF16)


def bias_unpack_kernel(perm_ref, parts_ref, out_ref):
    low = lax.broadcasted_iota(jnp.int32, (32, 128), 1) < 64
    for h in range(H):
        tops, bottoms = [], []
        for m in range(2):
            first = parts_ref[h * 4 + 2 * m, :32].astype(F32)
            second = parts_ref[h * 4 + 2 * m + 1, :32].astype(F32)
            tops.append(jnp.where(low, first, swap_halves(second)))
            bottoms.append(jnp.where(low, swap_halves(first), second))
        ordered = jnp.concatenate(
            [jnp.concatenate(tops, axis=1), jnp.concatenate(bottoms, axis=1)], axis=0
        ).astype(BF16)
        out_ref[h] = nt(ordered, perm_ref[...])


def project_kernel(
    pair_ref, grad_ref, wp_ref, wo_ref, send_a_ref, send_b_ref, gates_ref, ograd_ref
):
    wp = wp_ref[...]
    wo = wo_ref[...]
    group_p = lane_group(wp.shape)
    group_o = lane_group(wo.shape)
    zero = jnp.zeros((), BF16)
    wide_p = jnp.concatenate([jnp.where(group_p == r, wp, zero) for r in range(QUAD)], axis=0)
    wide_o = jnp.concatenate([jnp.where(group_o == r, wo, zero) for r in range(QUAD)], axis=0)

    def quads(ref):
        return jnp.concatenate(
            [
                jnp.concatenate([ref[4 * q + r] for r in range(QUAD)], axis=1)
                for q in range(4)
            ],
            axis=0,
        )

    proj = nn(quads(pair_ref), wide_p).astype(BF16)
    ograd = nn(quads(grad_ref), wide_o).astype(BF16)
    for q in range(4):
        rows = slice(q * TOK, (q + 1) * TOK)
        send_ref = send_b_ref if q // 2 else send_a_ref
        for h in range(H):
            query, key, value, gate = [
                proj[rows, h * 512 + p * 128 : h * 512 + (p + 1) * 128] for p in range(4)
            ]
            og = ograd[rows, h * 128 : (h + 1) * 128]
            gates_ref[q, :, h * 128 : (h + 1) * 128] = gate
            ograd_ref[q, :, h * 128 : (h + 1) * 128] = og
            cot = (og.astype(F32) * jax.nn.sigmoid(gate.astype(F32))).astype(BF16)
            for j in range(4):
                dest = (q % 2) * 16 + h * 4 + j
                send_ref[dest, :TOK] = value if j % 2 else key
                part = slice(j * SUB, (j + 1) * SUB)
                send_ref[dest, TOK : TOK + SUB] = query[part]
                send_ref[dest, TOK + SUB :] = cot[part]


CHUNK = 512
KEYS = 3 * LEN // 4


def attend_kernel(first, place_ref, chain_ref, recv_ref, other_ref, *refs):
    bias_refs, refs = refs[:8], refs[8:]
    if first:
        back_out, give_out, acc, *refs = refs
    else:
        acc_in, back_out, give_out, *refs = refs
        bg_outs, (acc, *refs) = refs[:5], refs[5:]
    b32, s_ref, kf, vf, kq, vq, kqt, vqt, dk, dv = refs
    yh, x, yl, core = place_ref[0], place_ref[1], place_ref[2], place_ref[4]
    low = lax.broadcasted_iota(jnp.int32, (32, 128), 1) < 64
    lens = [chain_ref[n] for n in range(CHAINS)]
    starts = [0, lens[0], lens[0] + lens[1], lens[0] + lens[1] + lens[2]]

    def place_of(chain, n):
        return starts[chain] + n * TOK

    def bias_piece(chain, a, b, c, n):
        if chain % 2:
            return bias_refs[4 + a][2 * b + c, n]
        return bias_refs[2 * b + c][a, n]

    def bias_grad_place(a, b):
        here, first_right, first_left, then_right, then_left = bg_outs
        return {
            (0, 0): (here, 0),
            (0, 1): (here, 2),
            (1, 0): (first_left, 0),
            (1, 1): (then_left, 0),
            (2, 0): (first_right, 0),
            (2, 1): (first_left, 2),
            (3, 0): (then_right, 0),
            (3, 1): (first_right, 2),
        }[a, b]

    def each_chain(body):
        for own in range(2):

            @pl.when(yl == own)
            def _(own=own):
                for chain in range(CHAINS):
                    step = functools.partial(body, chain, (chain // 2) ^ own)
                    lax.fori_loop(0, 8, step, 0, unroll=True)

    def build(chain, c, n, _):
        at = place_of(chain, n)
        for m in range(4):
            xs = 2 * (m % 2)
            left = bias_piece(chain, xs, m // 2, c, n).astype(F32) * LOG2E
            right = bias_piece(chain, xs + 1, m // 2, c, n).astype(F32) * LOG2E
            b32[m, pl.ds(at, 32), :] = jnp.where(low, left, swap_halves(right))
            b32[m, pl.ds(at + 32, 32), :] = jnp.where(low, swap_halves(left), right)
        t = chain * 8 + n
        mine = recv_ref[t, :TOK, :].astype(F32)
        theirs = other_ref[t].astype(F32)
        kf[pl.ds(at, TOK), :] = jnp.where(core == 0, mine, theirs)
        vf[pl.ds(at, TOK), :] = jnp.where(core == 0, theirs, mine)
        return 0

    each_chain(build)
    keys = kf[:KEYS, :].astype(BF16)
    values = vf[:KEYS, :].astype(BF16)
    kq[...] = keys
    vq[...] = values
    kqt[...] = keys.T
    vqt[...] = values.T

    homes = [((yh ^ (p // 4)) * 4 + ((x - p % 4) & 3)) * 4 for p in range(ROWS)]

    def queries(lo):
        return jnp.concatenate(
            [recv_ref[pl.ds(at, 4), lo : lo + SUB, :].reshape(TOK, 128) for at in homes], axis=0
        )

    query = queries(TOK)
    cot = queries(TOK + SUB)
    query_t = query.T
    cot_t = cot.T
    lanes = lane_group((QRY, 128))
    subs = lax.broadcasted_iota(jnp.int32, (128, QRY), 0) // D
    zero = jnp.zeros((), BF16)
    chunks = [slice(c * CHUNK, (c + 1) * CHUNK) for c in range(KEYS // CHUNK)]
    out_t, dq_t = [], []

    def operands(i):
        q_m = jnp.where(lanes == i, query, zero)
        c_m = jnp.where(lanes == i, cot, zero)
        qt_m = jnp.where(subs == i, query_t, zero)
        ct_m = jnp.where(subs == i, cot_t, zero)
        return q_m, c_m, qt_m, ct_m

    def score(i, rows, qt_m, top):
        s = nn(kq[rows, :], qt_m) * (SCALE * LOG2E)
        s = s + jnp.concatenate([b32[m, rows, :] for m in range(4)], axis=1)
        s_ref[i % 2, rows, :] = s
        return jnp.maximum(top, jnp.max(s.reshape(CHUNK // 8, 8, QRY), axis=0))

    lowest = jnp.full((8, QRY), -3e38, F32)
    ready = operands(0)
    top = lowest
    for rows in chunks:
        top = score(0, rows, ready[2], top)
    for i in range(QUAD):
        band = slice(i * D, (i + 1) * D)
        q_m, c_m, _, ct_m = ready
        top = jnp.max(top, axis=0, keepdims=True)
        total = jnp.zeros((8, QRY), F32)
        out = jnp.zeros((D, QRY), F32)
        for rows in chunks:
            e = jnp.exp2(s_ref[i % 2, rows, :] - top)
            s_ref[i % 2, rows, :] = e
            total = total + jnp.sum(e.reshape(CHUNK // 8, 8, QRY), axis=0)
            out = out + nn(vqt[band, rows], e.astype(BF16))
        inv = 1.0 / jnp.sum(total, axis=0, keepdims=True)
        out = out * inv
        delta = jnp.sum(cot_t[band].astype(F32) * out, axis=0, keepdims=True)
        dq = jnp.zeros((D, QRY), F32)
        if i + 1 < QUAD:
            ready = operands(i + 1)
            top = lowest
        for rows in chunks:
            if i + 1 < QUAD:
                top = score(i + 1, rows, ready[2], top)
            prob = s_ref[i % 2, rows, :] * inv
            ds = prob * (nn(vq[rows, :], ct_m) - delta)
            for m in range(4):
                part = ds[:, m * 128 : (m + 1) * 128]
                if i:
                    acc[m, rows, :] += part
                else:
                    acc[m, rows, :] = part if first else acc_in[m, rows, :] + part
            half = ds.astype(BF16)
            key_part = nn(half, q_m)
            value_part = nn(prob.astype(BF16), c_m)
            if i:
                dk[rows, :] += key_part
                dv[rows, :] += value_part
            else:
                dk[rows, :] = key_part
                dv[rows, :] = value_part
            dq = dq + nn(kqt[band, rows], half)
        out_t.append(out)
        dq_t.append(dq * SCALE)
    dq = jnp.concatenate(dq_t, axis=0).T.astype(BF16)
    out = jnp.concatenate(out_t, axis=0).T.astype(BF16)
    for p, at in enumerate(homes):
        part = slice(p * TOK, (p + 1) * TOK)
        back_out[pl.ds(at, 4), TOK : TOK + SUB, :] = dq[part].reshape(4, SUB, 128)
        back_out[pl.ds(at, 4), TOK + SUB :, :] = out[part].reshape(4, SUB, 128)

    def spread(chain, c, n, _):
        at = place_of(chain, n)
        here = lax.broadcasted_iota(jnp.int32, (TOK, 128), 0) < lens[chain] - n * TOK
        key_grad = jnp.where(here, dk[pl.ds(at, TOK), :] * SCALE, 0.0).astype(BF16)
        value_grad = jnp.where(here, dv[pl.ds(at, TOK), :], 0.0).astype(BF16)
        t = chain * 8 + n
        back_out[t, :TOK, :] = jnp.where(core == 0, key_grad, value_grad)
        give_out[t] = jnp.where(core == 0, value_grad, key_grad)
        if first:
            return 0
        for m in range(4):
            xs = 2 * (m % 2)
            top = jnp.where(here[:32], acc[m, pl.ds(at, 32), :], 0.0)
            bottom = jnp.where(here[32:], acc[m, pl.ds(at + 32, 32), :], 0.0)
            left = jnp.where(low, top, swap_halves(bottom))
            right = jnp.where(low, swap_halves(top), bottom)
            for a, value in ((xs, left), (xs + 1, right)):
                ref, base = bias_grad_place(a, m // 2)
                ref[base + c, (chain % 2) * 8 + n] = value.astype(BF16)
        return 0

    each_chain(spread)


def merge_kernel(back_ref, given_ref, out_ref):
    own = back_ref[:, :TOK, :].astype(F32)
    out_ref[:, :TOK, :] = (own + given_ref[...].astype(F32)).astype(BF16)
    out_ref[:, TOK:, :] = back_ref[:, TOK:, :]


def merge(back, given):
    return call(merge_kernel, [whole()] * 2, shape((COLS, CHUNK_ROWS, 128)), moved=2_000_000)(
        back, given
    )


def finish_kernel(part, recv_ref, gates_ref, ograd_ref, pair_ref, grad_ref, wp_ref, *refs):
    if part:
        weight_in, *bias_refs, pair_out, send_out, pg, gt, weight_out = refs
    else:
        pair_out, weight_out, pg, gt = refs
    quads = [2 * part, 2 * part + 1]
    for n, q in enumerate(quads):
        rows = slice(n * TOK, (n + 1) * TOK)
        for h in range(H):
            base = n * 16 + h * 4
            key = recv_ref[base, :TOK].astype(F32) + recv_ref[base + 2, :TOK].astype(F32)
            value = recv_ref[base + 1, :TOK].astype(F32) + recv_ref[base + 3, :TOK].astype(F32)
            query = jnp.concatenate(
                [recv_ref[base + j, TOK : TOK + SUB] for j in range(4)], axis=0
            )
            out = jnp.concatenate(
                [recv_ref[base + j, TOK + SUB :] for j in range(4)], axis=0
            ).astype(F32)
            lanes = slice(h * 128, (h + 1) * 128)
            sig = jax.nn.sigmoid(gates_ref[q, :, lanes].astype(F32))
            og = ograd_ref[q, :, lanes].astype(F32)
            gt[rows, lanes] = (sig * out).astype(BF16)
            pg[rows, h * 512 : h * 512 + 128] = query
            pg[rows, h * 512 + 128 : h * 512 + 256] = key.astype(BF16)
            pg[rows, h * 512 + 256 : h * 512 + 384] = value.astype(BF16)
            pg[rows, h * 512 + 384 : h * 512 + 512] = (og * out * sig * (1.0 - sig)).astype(BF16)
    wp = wp_ref[...]
    group = lane_group(wp.shape)
    zero = jnp.zeros((), BF16)
    grads = pg[...]
    gated = gt[...]
    for r in range(QUAD):
        pair_grad = nt(grads, jnp.where(group == r, wp, zero)).astype(BF16)
        for n in range(2):
            pair_out[4 * n + r] = pair_grad[n * TOK : (n + 1) * TOK]
    turned = grads.T
    gated_t = gated.T
    for r in range(QUAD):
        pair_r = jnp.concatenate([pair_ref[4 * q + r] for q in quads], axis=0)
        grad_r = jnp.concatenate([grad_ref[4 * q + r] for q in quads], axis=0)
        proj_part = nn(turned, pair_r)
        out_part = nn(gated_t, grad_r)
        for n in range(20):
            at = (n % 16) * 128 + r * D
            piece = (proj_part if n < 16 else out_part)[at : at + D] * (1.0 / LEN)
            rows = slice(n * D, (n + 1) * D)
            if r:
                weight_out[rows] += piece
            elif part:
                weight_out[rows] = weight_in[rows] + piece
            else:
                weight_out[rows] = piece
    if not part:
        return
    weight_out[640:] = jnp.zeros((128, 128), F32)
    bias_sum = bias_refs[0][...].astype(F32)
    for ref in bias_refs[1:]:
        bias_sum = bias_sum + ref[...].astype(F32)
    send_out[:, :32, :] = bias_sum.astype(BF16)
    send_out[:, 32:, :] = weight_out[...].astype(BF16).reshape(16, 48, 128)


def finish(part, home, gates, ograd, pair_rep, grad_out, wp, *more):
    last = shape((16, 80, 128)) if part else shape((640, 128), F32)
    scratch = [pltpu.VMEM((128, 2048), BF16), pltpu.VMEM((128, 512), BF16)]
    if part:
        scratch.append(pltpu.VMEM((768, 128), F32))
    return call(
        lambda *refs: finish_kernel(part, *refs),
        [whole()] * (6 + len(more)),
        (shape((8, TOK, 128)), last),
        scratch,
        flops=1_000_000_000,
        moved=3_000_000,
    )(home, gates, ograd, pair_rep, grad_out, wp, *more)


def whole():
    return pl.BlockSpec(memory_space=pltpu.VMEM)


def scalar():
    return pl.BlockSpec(memory_space=pltpu.SMEM)


def call(kernel, in_specs, outs, scratch=(), flops=0, moved=0):
    return pl.pallas_call(
        kernel,
        out_shape=outs,
        in_specs=in_specs,
        out_specs=jax.tree.map(lambda _: whole(), outs),
        scratch_shapes=list(scratch),
        compiler_params=pltpu.CompilerParams(vmem_limit_bytes=VMEM_LIMIT),
        cost_estimate=pl.CostEstimate(flops=flops, bytes_accessed=moved, transcendentals=0),
    )


def shape(dims, dtype=BF16):
    return jax.ShapeDtypeStruct(dims, dtype)


def query_order():
    perm = np.zeros((256, 256), np.float32)
    for s in range(4):
        for j in range(4):
            for t in range(SUB):
                perm[s * 64 + j * SUB + t, j * 64 + s * SUB + t] = 1.0
    return perm


def widen(groups):
    source = lax.broadcasted_iota(jnp.int32, (groups * D, groups * 128), 0)
    target = lax.broadcasted_iota(jnp.int32, (groups * D, groups * 128), 1)
    same = (source // D == target // 128) & (source % D == target % D)
    return same.astype(BF16)


def shift(x, axis, step):
    count = {"x": 4, "c": 2}[axis]
    return lax.ppermute(x, axis, [(n, (n + step) % count) for n in range(count)])


def flip_y(x, bits):
    return lax.ppermute(x, ("yh", "yl"), [(n, n ^ bits) for n in range(4)])


PIECE = (32, 128)
HALF = (2, 16) + PIECE
FULL = (4, 16) + PIECE


def gather_bias(own):
    even, odd = own[:8], own[8:]
    even = jnp.stack([even] + [shift(even, "x", n) for n in range(1, 4)])
    odd = jnp.stack([odd] + [flip_y(odd, n) for n in range(1, 4)])
    first = (even, odd)
    even = [even] + [flip_y(even, n) for n in range(1, 4)]
    odd = [odd] + [shift(odd, "x", n) for n in range(1, 4)]
    return even + odd, first


def total(*terms):
    return sum(t.astype(F32) for t in terms).astype(BF16)


def scatter_bias(parts):
    here, first_right, first_left, then_right, then_left = parts
    from_left = shift(first_right, "x", 1)
    from_right = shift(first_left, "x", -1)
    from_left_a = shift(total(then_right, from_left[:2]), "x", 1)
    from_right_b = shift(total(then_left, from_right[2:]), "x", -1)
    sum_a = total(here[:2], from_left_a, from_right[:2])
    sum_b = total(here[2:], from_right_b, from_left[2:])
    return sum_a[0], flip_y(sum_a[1], 1), flip_y(sum_b[0], 2), flip_y(sum_b[1], 3)


CHUNK_ROWS = TOK + 2 * SUB


def attend_call(first, place, chain_lengths, recv, other, bias, acc):
    packed = pltpu.VMEM((4, LEN, 128), F32)
    tall = [pltpu.VMEM((LEN, 128), F32)] * 2
    scratch = [packed, pltpu.VMEM((2, KEYS, QRY), F32)] + tall
    scratch += [pltpu.VMEM((KEYS, 128), BF16)] * 2 + [pltpu.VMEM((128, KEYS), BF16)] * 2 + tall
    outs = (shape((COLS, CHUNK_ROWS, 128)), shape((COLS, TOK, 128)))
    if first:
        outs += (shape((4, KEYS, 128), F32),)
    else:
        outs += (shape(FULL),) * 3 + (shape(HALF),) * 2
        scratch = [packed] + scratch
    return call(
        lambda *refs: attend_kernel(first, *refs),
        [scalar()] * 2 + [whole()] * (10 + len(acc)),
        outs,
        scratch,
        flops=25_000_000_000,
        moved=10_000_000,
    )(place, chain_lengths, recv, other, *bias, *acc)


def attend(first, place, chain_lengths, recv, bias, acc=()):
    other = shift(recv[:, :TOK], "c", 1)
    back, give, *rest = attend_call(first, place, chain_lengths, recv, other, bias, acc)
    given = shift(give, "c", 1)
    merged = merge(back, given)
    return merged, rest


def on_device(pair_rep, w_proj, bias_logits, chain_lengths, w_out, grad_out):
    col = ("yl", "z", "c")
    plane = ("yh", "x", "yl")
    line = ("z", "c")
    place = jnp.stack([lax.axis_index(a) for a in ("yh", "x", "yl", "z", "c")]).astype(jnp.int32)
    perm = jnp.asarray(query_order(), BF16)

    packed = call(
        bias_pack_kernel, [scalar(), scalar(), whole(), whole()], shape((16,) + PIECE)
    )(place, chain_lengths, perm, jnp.swapaxes(bias_logits, 1, 2))
    bias, first = gather_bias(lax.all_to_all(packed, line, 0, 0, tiled=True))
    wp = jnp.dot(w_proj, widen(16), preferred_element_type=F32).astype(BF16)
    wo = jnp.dot(w_out.T, widen(4), preferred_element_type=F32).astype(BF16)
    part = shape((COLS, CHUNK_ROWS, 128))
    send_a, send_b, gates, ograd = call(
        project_kernel,
        [whole()] * 4,
        (part, part, shape((4, TOK, 512)), shape((4, TOK, 512))),
        flops=700_000_000,
        moved=6_000_000,
    )(pair_rep, grad_out, wp, wo)
    recv_a = lax.all_to_all(send_a, col, 0, 0, tiled=True)
    recv_b = lax.all_to_all(send_b, col, 0, 0, tiled=True)
    recv_a, *first = lax.optimization_barrier((recv_a, *first))
    back_a, acc = attend(True, place, chain_lengths, recv_a, bias)
    home_a = lax.all_to_all(back_a, col, 0, 0, tiled=True)
    back_b, bg = attend(False, place, chain_lengths, recv_b, bias, acc)
    home_b = lax.all_to_all(back_b, col, 0, 0, tiled=True)
    shared = (gates, ograd, pair_rep, grad_out, wp)
    pair_a, weights = finish(0, home_a, *shared)
    pair_b, pieces = finish(1, home_b, *shared, weights, *scatter_bias(bg))
    pair_grad = jnp.concatenate([pair_a, pair_b], axis=0)
    pieces = lax.all_to_all(pieces, line, 0, 0, tiled=True)
    bias_grad = call(bias_unpack_kernel, [whole()] * 2, shape((H, TOK, 256), F32))(perm, pieces)
    share = jnp.sum(pieces[:, 32:].astype(F32), axis=0)
    share = lax.all_to_all(
        jnp.broadcast_to(share.astype(BF16)[None], (16, 48, 128)), plane, 0, 0, tiled=True
    )
    share = jnp.sum(share.astype(F32), axis=0).astype(BF16)
    every = lax.all_to_all(
        jnp.broadcast_to(share[None], (16, 48, 128)), line, 0, 0, tiled=True
    )
    every = every.reshape(768, 128).astype(F32)
    return (pair_grad, jnp.swapaxes(bias_grad, 1, 2), every[:512].T, every[512:640])


def solution(mesh):
    fine = Mesh(mesh.devices.reshape(2, 4, 2, 8, 2), ("yh", "x", "yl", "z", "c"))
    row = ("yh", "x")
    col = ("yl", "z", "c")
    return jax.shard_map(
        on_device,
        mesh=fine,
        in_specs=(
            P(row, col, None),
            P(),
            P(None, row, col),
            P(),
            P(),
            P(row, col, None),
        ),
        out_specs=(P(row, col, None), P(None, row, col), P(), P()),
        check_vma=False,
    )
```

```python
import functools

import jax
import jax.numpy as jnp
import numpy as np
from jax import lax
from jax.experimental import pallas as pl
from jax.experimental.pallas import tpu as pltpu
from jax.sharding import Mesh
from jax.sharding import PartitionSpec as P

H = 4
D = 32
CHAINS = 4
NEG_BIG = -1e30
LOG2E = 1.4426950408889634
SCALE = D ** (-0.5)
F32 = jnp.float32
BF16 = jnp.bfloat16
QUAD = 4
TOK = 64
SUB = 16
COLS = 32
ROWS = 8
LEN = TOK * COLS
QRY = SUB * COLS
VMEM_LIMIT = 56 * 1024 * 1024


def dot(a, b, dims):
    return lax.dot_general(a, b, (dims, ((), ())), preferred_element_type=F32)


def nn(a, b):
    return dot(a, b, ((1,), (0,)))


def nt(a, b):
    return dot(a, b, ((1,), (1,)))


def tn(a, b):
    return dot(a, b, ((0,), (0,)))


def lane_group(shape):
    return (lax.broadcasted_iota(jnp.int32, shape, 1) // D) % QUAD


def swap_halves(x):
    return jnp.concatenate([x[:, TOK:], x[:, :TOK]], axis=1)


def bias_pack_kernel(place_ref, chain_ref, perm_ref, bias_ref, out_ref):
    block = (place_ref[2] * 8 + place_ref[3]) * 2 + place_ref[4]
    per_chain = COLS // CHAINS
    limit = chain_ref[block // per_chain] - (block % per_chain) * TOK
    low = lax.broadcasted_iota(jnp.int32, (32, 128), 1) < 64
    valid = lax.broadcasted_iota(jnp.int32, (TOK, 256), 0) < limit
    for h in range(H):
        ordered = jnp.where(valid, nn(bias_ref[h], perm_ref[...]), NEG_BIG)
        for m in range(2):
            top = ordered[:32, m * 128 : (m + 1) * 128]
            bottom = ordered[32:, m * 128 : (m + 1) * 128]
            out_ref[h * 4 + 2 * m] = jnp.where(low, top, swap_halves(bottom)).astype(BF16)
            out_ref[h * 4 + 2 * m + 1] = jnp.where(low, swap_halves(top), bottom).astype(BF16)


def bias_unpack_kernel(perm_ref, parts_ref, out_ref):
    low = lax.broadcasted_iota(jnp.int32, (32, 128), 1) < 64
    for h in range(H):
        tops, bottoms = [], []
        for m in range(2):
            first = parts_ref[h * 4 + 2 * m, :32].astype(F32)
            second = parts_ref[h * 4 + 2 * m + 1, :32].astype(F32)
            tops.append(jnp.where(low, first, swap_halves(second)))
            bottoms.append(jnp.where(low, swap_halves(first), second))
        ordered = jnp.concatenate(
            [jnp.concatenate(tops, axis=1), jnp.concatenate(bottoms, axis=1)], axis=0
        ).astype(BF16)
        out_ref[h] = nt(ordered, perm_ref[...])


def project_kernel(
    pair_ref, grad_ref, wp_ref, wo_ref, send_a_ref, send_b_ref, gates_ref, ograd_ref
):
    wp = wp_ref[...]
    wo = wo_ref[...]
    group_p = lane_group(wp.shape)
    group_o = lane_group(wo.shape)
    zero = jnp.zeros((), BF16)
    wide_p = jnp.concatenate([jnp.where(group_p == r, wp, zero) for r in range(QUAD)], axis=0)
    wide_o = jnp.concatenate([jnp.where(group_o == r, wo, zero) for r in range(QUAD)], axis=0)

    def quads(ref):
        return jnp.concatenate(
            [
                jnp.concatenate([ref[4 * q + r] for r in range(QUAD)], axis=1)
                for q in range(4)
            ],
            axis=0,
        )

    proj = nn(quads(pair_ref), wide_p).astype(BF16)
    ograd = nn(quads(grad_ref), wide_o).astype(BF16)
    for q in range(4):
        rows = slice(q * TOK, (q + 1) * TOK)
        send_ref = send_b_ref if q // 2 else send_a_ref
        for h in range(H):
            query, key, value, gate = [
                proj[rows, h * 512 + p * 128 : h * 512 + (p + 1) * 128] for p in range(4)
            ]
            og = ograd[rows, h * 128 : (h + 1) * 128]
            gates_ref[q, :, h * 128 : (h + 1) * 128] = gate
            ograd_ref[q, :, h * 128 : (h + 1) * 128] = og
            cot = (og.astype(F32) * jax.nn.sigmoid(gate.astype(F32))).astype(BF16)
            for j in range(4):
                dest = (q % 2) * 16 + h * 4 + j
                send_ref[dest, :TOK] = value if j % 2 else key
                part = slice(j * SUB, (j + 1) * SUB)
                send_ref[dest, TOK : TOK + SUB] = query[part]
                send_ref[dest, TOK + SUB :] = cot[part]


CHUNK = 512
KEYS = 3 * LEN // 4


def attend_kernel(first, place_ref, chain_ref, recv_ref, other_ref, *refs):
    bias_refs, refs = refs[:8], refs[8:]
    if first:
        back_out, give_out, acc, *refs = refs
    else:
        acc_in, back_out, give_out, *refs = refs
        bg_outs, (acc, *refs) = refs[:5], refs[5:]
    b32, s_ref, kf, vf, kq, vq, kqt, vqt, dk, dv = refs
    yh, x, yl, core = place_ref[0], place_ref[1], place_ref[2], place_ref[4]
    low = lax.broadcasted_iota(jnp.int32, (32, 128), 1) < 64
    lens = [chain_ref[n] for n in range(CHAINS)]
    starts = [0, lens[0], lens[0] + lens[1], lens[0] + lens[1] + lens[2]]

    def place_of(chain, n):
        return starts[chain] + n * TOK

    def bias_piece(chain, a, b, c, n):
        if chain % 2:
            return bias_refs[4 + a][2 * b + c, n]
        return bias_refs[2 * b + c][a, n]

    def bias_grad_place(a, b):
        here, first_right, first_left, then_right, then_left = bg_outs
        return {
            (0, 0): (here, 0),
            (0, 1): (here, 2),
            (1, 0): (first_left, 0),
            (1, 1): (then_left, 0),
            (2, 0): (first_right, 0),
            (2, 1): (first_left, 2),
            (3, 0): (then_right, 0),
            (3, 1): (first_right, 2),
        }[a, b]

    def each_chain(body):
        for own in range(2):

            @pl.when(yl == own)
            def _(own=own):
                for chain in range(CHAINS):
                    step = functools.partial(body, chain, (chain // 2) ^ own)
                    lax.fori_loop(0, 8, step, 0, unroll=True)

    def build(chain, c, n, _):
        at = place_of(chain, n)
        for m in range(4):
            xs = 2 * (m % 2)
            left = bias_piece(chain, xs, m // 2, c, n).astype(F32) * LOG2E
            right = bias_piece(chain, xs + 1, m // 2, c, n).astype(F32) * LOG2E
            b32[m, pl.ds(at, 32), :] = jnp.where(low, left, swap_halves(right))
            b32[m, pl.ds(at + 32, 32), :] = jnp.where(low, swap_halves(left), right)
        t = chain * 8 + n
        mine = recv_ref[t, :TOK, :].astype(F32)
        theirs = other_ref[t].astype(F32)
        kf[pl.ds(at, TOK), :] = jnp.where(core == 0, mine, theirs)
        vf[pl.ds(at, TOK), :] = jnp.where(core == 0, theirs, mine)
        return 0

    each_chain(build)
    keys = kf[:KEYS, :].astype(BF16)
    values = vf[:KEYS, :].astype(BF16)
    kq[...] = keys
    vq[...] = values
    kqt[...] = keys.T
    vqt[...] = values.T

    homes = [((yh ^ (p // 4)) * 4 + ((x - p % 4) & 3)) * 4 for p in range(ROWS)]

    def queries(lo):
        return jnp.concatenate(
            [recv_ref[pl.ds(at, 4), lo : lo + SUB, :].reshape(TOK, 128) for at in homes], axis=0
        )

    query = queries(TOK)
    cot = queries(TOK + SUB)
    query_t = query.T
    cot_t = cot.T
    lanes = lane_group((QRY, 128))
    subs = lax.broadcasted_iota(jnp.int32, (128, QRY), 0) // D
    zero = jnp.zeros((), BF16)
    chunks = [slice(c * CHUNK, (c + 1) * CHUNK) for c in range(KEYS // CHUNK)]
    out_t, dq_t = [], []

    def operands(i):
        q_m = jnp.where(lanes == i, query, zero)
        c_m = jnp.where(lanes == i, cot, zero)
        qt_m = jnp.where(subs == i, query_t, zero)
        ct_m = jnp.where(subs == i, cot_t, zero)
        return q_m, c_m, qt_m, ct_m

    def score(i, rows, qt_m, top):
        s = nn(kq[rows, :], qt_m) * (SCALE * LOG2E)
        s = s + jnp.concatenate([b32[m, rows, :] for m in range(4)], axis=1)
        s_ref[i % 2, rows, :] = s
        return jnp.maximum(top, jnp.max(s.reshape(CHUNK // 8, 8, QRY), axis=0))

    lowest = jnp.full((8, QRY), -3e38, F32)
    ready = operands(0)
    top = lowest
    for rows in chunks:
        top = score(0, rows, ready[2], top)
    for i in range(QUAD):
        band = slice(i * D, (i + 1) * D)
        q_m, c_m, _, ct_m = ready
        top = jnp.max(top, axis=0, keepdims=True)
        total = jnp.zeros((8, QRY), F32)
        out = jnp.zeros((D, QRY), F32)
        for rows in chunks:
            e = jnp.exp2(s_ref[i % 2, rows, :] - top)
            s_ref[i % 2, rows, :] = e
            total = total + jnp.sum(e.reshape(CHUNK // 8, 8, QRY), axis=0)
            out = out + nn(vqt[band, rows], e.astype(BF16))
        inv = 1.0 / jnp.sum(total, axis=0, keepdims=True)
        out = out * inv
        delta = jnp.sum(cot_t[band].astype(F32) * out, axis=0, keepdims=True)
        dq = jnp.zeros((D, QRY), F32)
        if i + 1 < QUAD:
            ready = operands(i + 1)
            top = lowest
        for rows in chunks:
            if i + 1 < QUAD:
                top = score(i + 1, rows, ready[2], top)
            prob = s_ref[i % 2, rows, :] * inv
            ds = prob * (nn(vq[rows, :], ct_m) - delta)
            for m in range(4):
                part = ds[:, m * 128 : (m + 1) * 128]
                if i:
                    acc[m, rows, :] += part
                else:
                    acc[m, rows, :] = part if first else acc_in[m, rows, :] + part
            half = ds.astype(BF16)
            key_part = nn(half, q_m)
            value_part = nn(prob.astype(BF16), c_m)
            if i:
                dk[rows, :] += key_part
                dv[rows, :] += value_part
            else:
                dk[rows, :] = key_part
                dv[rows, :] = value_part
            dq = dq + nn(kqt[band, rows], half)
        out_t.append(out)
        dq_t.append(dq * SCALE)
    dq = jnp.concatenate(dq_t, axis=0).T.astype(BF16)
    out = jnp.concatenate(out_t, axis=0).T.astype(BF16)
    for p, at in enumerate(homes):
        part = slice(p * TOK, (p + 1) * TOK)
        back_out[pl.ds(at, 4), TOK : TOK + SUB, :] = dq[part].reshape(4, SUB, 128)
        back_out[pl.ds(at, 4), TOK + SUB :, :] = out[part].reshape(4, SUB, 128)

    def spread(chain, c, n, _):
        at = place_of(chain, n)
        here = lax.broadcasted_iota(jnp.int32, (TOK, 128), 0) < lens[chain] - n * TOK
        key_grad = jnp.where(here, dk[pl.ds(at, TOK), :] * SCALE, 0.0).astype(BF16)
        value_grad = jnp.where(here, dv[pl.ds(at, TOK), :], 0.0).astype(BF16)
        t = chain * 8 + n
        back_out[t, :TOK, :] = jnp.where(core == 0, key_grad, value_grad)
        give_out[t] = jnp.where(core == 0, value_grad, key_grad)
        if first:
            return 0
        for m in range(4):
            xs = 2 * (m % 2)
            top = jnp.where(here[:32], acc[m, pl.ds(at, 32), :], 0.0)
            bottom = jnp.where(here[32:], acc[m, pl.ds(at + 32, 32), :], 0.0)
            left = jnp.where(low, top, swap_halves(bottom))
            right = jnp.where(low, swap_halves(top), bottom)
            for a, value in ((xs, left), (xs + 1, right)):
                ref, base = bias_grad_place(a, m // 2)
                ref[base + c, (chain % 2) * 8 + n] = value.astype(BF16)
        return 0

    each_chain(spread)


def merge_kernel(back_ref, given_ref, out_ref):
    own = back_ref[:, :TOK, :].astype(F32)
    out_ref[:, :TOK, :] = (own + given_ref[...].astype(F32)).astype(BF16)
    out_ref[:, TOK:, :] = back_ref[:, TOK:, :]


def merge(back, given):
    return call(merge_kernel, [whole()] * 2, shape((COLS, CHUNK_ROWS, 128)), moved=2_000_000)(
        back, given
    )


def finish_kernel(part, recv_ref, gates_ref, ograd_ref, pair_ref, grad_ref, *refs):
    if part:
        weight_in, *bias_refs, pg, send_out, gt, weight_out = refs
    else:
        pg, weight_out, gt = refs
    quads = [2 * part, 2 * part + 1]
    for n, q in enumerate(quads):
        rows = slice(n * TOK, (n + 1) * TOK)
        for h in range(H):
            base = n * 16 + h * 4
            key = recv_ref[base, :TOK].astype(F32) + recv_ref[base + 2, :TOK].astype(F32)
            value = recv_ref[base + 1, :TOK].astype(F32) + recv_ref[base + 3, :TOK].astype(F32)
            query = jnp.concatenate(
                [recv_ref[base + j, TOK : TOK + SUB] for j in range(4)], axis=0
            )
            out = jnp.concatenate(
                [recv_ref[base + j, TOK + SUB :] for j in range(4)], axis=0
            ).astype(F32)
            lanes = slice(h * 128, (h + 1) * 128)
            sig = jax.nn.sigmoid(gates_ref[q, :, lanes].astype(F32))
            og = ograd_ref[q, :, lanes].astype(F32)
            gt[rows, lanes] = (sig * out).astype(BF16)
            pg[rows, h * 512 : h * 512 + 128] = query
            pg[rows, h * 512 + 128 : h * 512 + 256] = key.astype(BF16)
            pg[rows, h * 512 + 256 : h * 512 + 384] = value.astype(BF16)
            pg[rows, h * 512 + 384 : h * 512 + 512] = (og * out * sig * (1.0 - sig)).astype(BF16)
    grads = pg[...]
    gated = gt[...]
    turned = grads.T
    gated_t = gated.T
    for r in range(QUAD):
        pair_r = jnp.concatenate([pair_ref[4 * q + r] for q in quads], axis=0)
        grad_r = jnp.concatenate([grad_ref[4 * q + r] for q in quads], axis=0)
        proj_part = nn(turned, pair_r)
        out_part = nn(gated_t, grad_r)
        for n in range(20):
            at = (n % 16) * 128 + r * D
            piece = (proj_part if n < 16 else out_part)[at : at + D] * (1.0 / LEN)
            rows = slice(n * D, (n + 1) * D)
            if r:
                weight_out[rows] += piece
            elif part:
                weight_out[rows] = weight_in[rows] + piece
            else:
                weight_out[rows] = piece
    if not part:
        return
    weight_out[640:] = jnp.zeros((128, 128), F32)
    bias_sum = bias_refs[0][...].astype(F32)
    for ref in bias_refs[1:]:
        bias_sum = bias_sum + ref[...].astype(F32)
    send_out[:, :32, :] = bias_sum.astype(BF16)
    send_out[:, 32:, :] = weight_out[...].astype(BF16).reshape(16, 48, 128)


def pair_kernel(grads_a_ref, grads_b_ref, wp_ref, pair_out):
    wp = wp_ref[...]
    group = lane_group(wp.shape)
    zero = jnp.zeros((), BF16)
    grads = jnp.concatenate([grads_a_ref[...], grads_b_ref[...]], axis=0)
    for r in range(QUAD):
        pair_grad = nt(grads, jnp.where(group == r, wp, zero)).astype(BF16)
        for q in range(4):
            pair_out[4 * q + r] = pair_grad[q * TOK : (q + 1) * TOK]


def finish(part, home, gates, ograd, pair_rep, grad_out, *more):
    last = shape((16, 80, 128)) if part else shape((640, 128), F32)
    scratch = [pltpu.VMEM((128, 512), BF16)]
    if part:
        scratch.append(pltpu.VMEM((768, 128), F32))
    return call(
        lambda *refs: finish_kernel(part, *refs),
        [whole()] * (5 + len(more)),
        (shape((128, 2048)), last),
        scratch,
        flops=500_000_000,
        moved=3_000_000,
    )(home, gates, ograd, pair_rep, grad_out, *more)


def whole():
    return pl.BlockSpec(memory_space=pltpu.VMEM)


def scalar():
    return pl.BlockSpec(memory_space=pltpu.SMEM)


def call(kernel, in_specs, outs, scratch=(), flops=0, moved=0):
    return pl.pallas_call(
        kernel,
        out_shape=outs,
        in_specs=in_specs,
        out_specs=jax.tree.map(lambda _: whole(), outs),
        scratch_shapes=list(scratch),
        compiler_params=pltpu.CompilerParams(vmem_limit_bytes=VMEM_LIMIT),
        cost_estimate=pl.CostEstimate(flops=flops, bytes_accessed=moved, transcendentals=0),
    )


def shape(dims, dtype=BF16):
    return jax.ShapeDtypeStruct(dims, dtype)


def query_order():
    perm = np.zeros((256, 256), np.float32)
    for s in range(4):
        for j in range(4):
            for t in range(SUB):
                perm[s * 64 + j * SUB + t, j * 64 + s * SUB + t] = 1.0
    return perm


def widen(groups):
    source = lax.broadcasted_iota(jnp.int32, (groups * D, groups * 128), 0)
    target = lax.broadcasted_iota(jnp.int32, (groups * D, groups * 128), 1)
    same = (source // D == target // 128) & (source % D == target % D)
    return same.astype(BF16)


def shift(x, axis, step):
    count = {"x": 4, "c": 2}[axis]
    return lax.ppermute(x, axis, [(n, (n + step) % count) for n in range(count)])


def flip_y(x, bits):
    return lax.ppermute(x, ("yh", "yl"), [(n, n ^ bits) for n in range(4)])


PIECE = (32, 128)
HALF = (2, 16) + PIECE
FULL = (4, 16) + PIECE


def gather_bias(own):
    even, odd = own[:8], own[8:]
    even = jnp.stack([even] + [shift(even, "x", n) for n in range(1, 4)])
    odd = jnp.stack([odd] + [flip_y(odd, n) for n in range(1, 4)])
    first = (even, odd)
    even = [even] + [flip_y(even, n) for n in range(1, 4)]
    odd = [odd] + [shift(odd, "x", n) for n in range(1, 4)]
    return even + odd, first


def total(*terms):
    return sum(t.astype(F32) for t in terms).astype(BF16)


def scatter_bias(parts):
    here, first_right, first_left, then_right, then_left = parts
    from_left = shift(first_right, "x", 1)
    from_right = shift(first_left, "x", -1)
    from_left_a = shift(total(then_right, from_left[:2]), "x", 1)
    from_right_b = shift(total(then_left, from_right[2:]), "x", -1)
    sum_a = total(here[:2], from_left_a, from_right[:2])
    sum_b = total(here[2:], from_right_b, from_left[2:])
    return sum_a[0], flip_y(sum_a[1], 1), flip_y(sum_b[0], 2), flip_y(sum_b[1], 3)


CHUNK_ROWS = TOK + 2 * SUB


def attend_call(first, place, chain_lengths, recv, other, bias, acc):
    packed = pltpu.VMEM((4, LEN, 128), F32)
    tall = [pltpu.VMEM((LEN, 128), F32)] * 2
    scratch = [packed, pltpu.VMEM((2, KEYS, QRY), F32)] + tall
    scratch += [pltpu.VMEM((KEYS, 128), BF16)] * 2 + [pltpu.VMEM((128, KEYS), BF16)] * 2 + tall
    outs = (shape((COLS, CHUNK_ROWS, 128)), shape((COLS, TOK, 128)))
    if first:
        outs += (shape((4, KEYS, 128), F32),)
    else:
        outs += (shape(FULL),) * 3 + (shape(HALF),) * 2
        scratch = [packed] + scratch
    return call(
        lambda *refs: attend_kernel(first, *refs),
        [scalar()] * 2 + [whole()] * (10 + len(acc)),
        outs,
        scratch,
        flops=25_000_000_000,
        moved=10_000_000,
    )(place, chain_lengths, recv, other, *bias, *acc)


def attend(first, place, chain_lengths, recv, bias, acc=()):
    other = shift(recv[:, :TOK], "c", 1)
    back, give, *rest = attend_call(first, place, chain_lengths, recv, other, bias, acc)
    given = shift(give, "c", 1)
    merged = merge(back, given)
    return merged, rest


def on_device(pair_rep, w_proj, bias_logits, chain_lengths, w_out, grad_out):
    col = ("yl", "z", "c")
    plane = ("yh", "x", "yl")
    line = ("z", "c")
    place = jnp.stack([lax.axis_index(a) for a in ("yh", "x", "yl", "z", "c")]).astype(jnp.int32)
    perm = jnp.asarray(query_order(), BF16)

    packed = call(
        bias_pack_kernel, [scalar(), scalar(), whole(), whole()], shape((16,) + PIECE)
    )(place, chain_lengths, perm, jnp.swapaxes(bias_logits, 1, 2))
    bias, first = gather_bias(lax.all_to_all(packed, line, 0, 0, tiled=True))
    wp = jnp.dot(w_proj, widen(16), preferred_element_type=F32).astype(BF16)
    wo = jnp.dot(w_out.T, widen(4), preferred_element_type=F32).astype(BF16)
    part = shape((COLS, CHUNK_ROWS, 128))
    send_a, send_b, gates, ograd = call(
        project_kernel,
        [whole()] * 4,
        (part, part, shape((4, TOK, 512)), shape((4, TOK, 512))),
        flops=700_000_000,
        moved=6_000_000,
    )(pair_rep, grad_out, wp, wo)
    recv_a = lax.all_to_all(send_a, col, 0, 0, tiled=True)
    recv_b = lax.all_to_all(send_b, col, 0, 0, tiled=True)
    recv_a, *first = lax.optimization_barrier((recv_a, *first))
    back_a, acc = attend(True, place, chain_lengths, recv_a, bias)
    home_a = lax.all_to_all(back_a, col, 0, 0, tiled=True)
    back_b, bg = attend(False, place, chain_lengths, recv_b, bias, acc)
    home_b = lax.all_to_all(back_b, col, 0, 0, tiled=True)
    shared = (gates, ograd, pair_rep, grad_out)
    grads_a, weights = finish(0, home_a, *shared)
    grads_b, pieces = finish(1, home_b, *shared, weights, *scatter_bias(bg))
    pair_grad = call(
        pair_kernel,
        [whole()] * 3,
        shape((16, TOK, 128)),
        flops=1_000_000_000,
        moved=3_000_000,
    )(grads_a, grads_b, wp)
    pieces = lax.all_to_all(pieces, line, 0, 0, tiled=True)
    bias_grad = call(bias_unpack_kernel, [whole()] * 2, shape((H, TOK, 256), F32))(perm, pieces)
    share = jnp.sum(pieces[:, 32:].astype(F32), axis=0)
    share = lax.all_to_all(
        jnp.broadcast_to(share.astype(BF16)[None], (16, 48, 128)), plane, 0, 0, tiled=True
    )
    share = jnp.sum(share.astype(F32), axis=0).astype(BF16)
    every = lax.all_to_all(
        jnp.broadcast_to(share[None], (16, 48, 128)), line, 0, 0, tiled=True
    )
    every = every.reshape(768, 128).astype(F32)
    return (pair_grad, jnp.swapaxes(bias_grad, 1, 2), every[:512].T, every[512:640])


def solution(mesh):
    fine = Mesh(mesh.devices.reshape(2, 4, 2, 8, 2), ("yh", "x", "yl", "z", "c"))
    row = ("yh", "x")
    col = ("yl", "z", "c")
    return jax.shard_map(
        on_device,
        mesh=fine,
        in_specs=(
            P(row, col, None),
            P(),
            P(None, row, col),
            P(),
            P(),
            P(row, col, None),
        ),
        out_specs=(P(row, col, None), P(None, row, col), P(), P()),
        check_vma=False,
    )
```
